32 devices in a mesh: grp: 4 (over y, x), dev: 8 (over z, core).
Axes of the slice: x: 2, y: 2, z: 4, core: 2. Of those that a mesh axis runs over, the one named last changes fastest.
Arguments:
- positions: float32 [3, 8192], P(None, ('grp', 'dev')), may hold values from -1 to 1
- velocities: float32 [3, 8192], P(None, ('grp', 'dev')), may hold values from -4 to 4
- accel_old: float32 [3, 8192], P(None, ('grp', 'dev')), may hold values from -6 to 6
- jerk_old: float32 [3, 8192], P(None, ('grp', 'dev')), may hold values from -6 to 6
- masses: float32 [8192], P(('grp', 'dev')), may hold values from 2.4414063e-05 to 0.00061035156
- levels: int32 [8192], P(('grp', 'dev')), may hold values from 0 to 3
- live_count: int32 [32], P(('grp', 'dev')), may hold values from 128 to 256, as said below
- active_slot: int32 [4096], P(('grp', 'dev')), may hold values from 0 to 255, as said below
Outputs:
- pos_vel: float32 [6, 4096], P(None, ('grp', 'dev'))
- acc_jerk: float32 [6, 4096], P(None, ('grp', 'dev'))
- potential: float32 [4096], P(('grp', 'dev'))
The draws below stay inside these ranges and needn't reach their ends.
Inputs may be any that keep to these rules, and one draw needn't show every extreme that they name: `live_count`: every entry is at least 128; some device is full with 256 and some has exactly 128; the counts are uneven across devices. `active_slot`: within each device's aligned block of 128 entries the slots are distinct and below that device's live_count.
All inputs are finite; a program needn't handle non-finite values.
Results may differ from the reference program's by a relative error of at most 0.00029.
Values sent between devices are 32-bit elements; how exact they have to be, the bound alone decides.
A program may use at most 64 MiB of HBM per device.

```python
import math
import jax
import jax.numpy as jnp
from jax import lax

SRC_DEV = 256
ACT_DEV = 128
LEVELS = 4
SOURCES = 8192
NACT = 4096
DEVICES = 32


def live_counts_helper(key):
    base = jax.random.fold_in(key, 11)
    roll = jax.random.randint(base, (DEVICES,), 0, 33)
    counts = ACT_DEV + (SRC_DEV - ACT_DEV) * roll * roll // 1024
    full_device = jax.random.randint(jax.random.fold_in(key, 12), (), 0, DEVICES)
    counts = counts.at[full_device].set(SRC_DEV)
    counts = counts.at[(full_device + 1) % DEVICES].set(ACT_DEV)
    return counts.astype(jnp.int32)


def draw_live_count(key, part):
    return live_counts_helper(key)


def draw_active_slot(key, part):
    counts = live_counts_helper(key)
    column = jnp.arange(SRC_DEV, dtype=jnp.int32)[None, :]
    scores = jax.random.randint(jax.random.fold_in(key, 13), (DEVICES, SRC_DEV), 0, 2 ** 19) * SRC_DEV + column
    scores = scores + (column >= counts[:, None]).astype(jnp.int32) * 2 ** 30
    first = (column == SRC_DEV - 1) & (counts[:, None] == SRC_DEV)
    scores = jnp.where(first, -1, scores)
    order = jnp.argsort(scores, axis=1, stable=True)[:, :ACT_DEV]
    return order.reshape(-1).astype(jnp.int32)


def touch_ends(array, stream_key, smallest, largest):
    longest = array.shape.index(max(array.shape))
    spots = []
    for shift in (0, 1):
        where = [jax.random.randint(jax.random.fold_in(stream_key, axis), (), 0, length) for axis, length in enumerate(array.shape)]
        where[longest] = (where[longest] + shift) % array.shape[longest]
        spots.append(tuple(where))
    return array.at[spots[0]].set(smallest).at[spots[1]].set(largest)


def shard_levels(stream_key, extent, split, smallest, high):
    def one(position, blocks):
        heights = jax.random.uniform(jax.random.fold_in(jax.random.fold_in(stream_key, 6), position), (blocks,), jnp.float32, smallest / len(split), high / len(split))
        return jnp.repeat(jnp.exp(heights), extent[position] // blocks).reshape((-1,) + (1,) * (len(extent) - position - 1))

    gain = one(*split[0])
    for cut in split[1:]:
        gain = gain * one(*cut)
    return gain


def centred(key, dims, deviation, limit, cuts=(), kind=jnp.bfloat16):
    gain = shard_levels(key, dims, cuts, -0.22, 0.18) if cuts else 1.0
    drawn = jax.random.normal(key, dims, jnp.float32) * deviation * gain
    return jnp.minimum(jnp.maximum(drawn, -limit), limit).astype(kind)


def setup_inputs(seed: int = 0) -> dict:
    keys = jax.random.split(jax.random.key(seed), 9)
    return {
        "positions": jnp.clip(jax.random.uniform(keys[0], (3, SOURCES), jnp.float32, -1.0, 1.0) * shard_levels(keys[0], (3, SOURCES), ((1, 32),), -0.4, 0.0), -1.0, 1.0),
        "velocities": centred(keys[1], (3, SOURCES), 0.5, 4.0, ((1, 32),), jnp.float32),
        "accel_old": centred(keys[2], (3, SOURCES), 1.0, 6.0, ((1, 32),), jnp.float32),
        "jerk_old": centred(keys[3], (3, SOURCES), 1.0, 6.0, ((1, 32),), jnp.float32),
        "masses": jnp.clip(jnp.exp(math.log(0.00061035156) - 3.218876 * jax.random.uniform(keys[4], (SOURCES,), jnp.float32) ** shard_levels(keys[4], (SOURCES,), ((0, 32),), -0.2, 0.2)), 2.441406286379788e-05, 0.00061035156),
        "levels": touch_ends(jax.random.randint(keys[5], (SOURCES,), 0, LEVELS), jax.random.fold_in(keys[5], 1), 0, LEVELS - 1).astype(jnp.int32),
        "live_count": draw_live_count(jax.random.fold_in(keys[8], 71), 0),
        "active_slot": draw_active_slot(jax.random.fold_in(keys[8], 71), 0),
    }


tau_base = 0.5
soften_sq = 0.0001

def pair_terms(active_state, src_pos, src_vel, src_mass):
    delta_pos = src_pos[:, None, :] - active_state[0:3, :, None]
    delta_vel = src_vel[:, None, :] - active_state[3:6, :, None]
    dist_sq = lax.optimization_barrier(jnp.sum(delta_pos * delta_pos, axis=0)) + soften_sq
    weight = src_mass[None, :] / jnp.sqrt(dist_sq)
    cubed = weight / dist_sq
    radial = 3.0 * lax.optimization_barrier(jnp.sum(delta_pos * delta_vel, axis=0)) / dist_sq
    accel = lax.optimization_barrier(jnp.sum(cubed[None] * delta_pos, axis=2))
    jerk_new = lax.optimization_barrier(jnp.sum(cubed[None] * (delta_vel - radial[None] * delta_pos), axis=2))
    pot_sum = -lax.optimization_barrier(jnp.sum(weight, axis=1))
    return jnp.concatenate([accel, jerk_new, pot_sum[None]], axis=0)

def correct(state, summed):
    pos_now = state[0:3]
    vel_now = state[3:6]
    acc_start = state[6:9]
    jerk_start = state[9:12]
    step_size = state[12:13]
    acc_end = summed[0:3]
    jerk_end = summed[3:6]
    differ = acc_start - acc_end
    fourth = -6.0 * differ - step_size * (4.0 * jerk_start + 2.0 * jerk_end)
    fifth = 12.0 * differ + 6.0 * step_size * (jerk_start + jerk_end)
    new_pos = pos_now + step_size * step_size / 24.0 * fourth + step_size * step_size / 120.0 * fifth
    new_vel = vel_now + step_size / 6.0 * fourth + step_size / 24.0 * fifth
    return (jnp.concatenate([new_pos, new_vel], axis=0), summed[0:6], summed[6])

def reference(positions, velocities, accel_old, jerk_old, masses, levels, live_count, active_slot):
    elapsed = tau_base * jnp.exp2(-levels.astype(jnp.float32))
    pos_pred = positions + elapsed * (velocities + elapsed * (accel_old / 2.0 + elapsed * jerk_old / 6.0))
    vel_pred = velocities + elapsed * (accel_old + elapsed * jerk_old / 2.0)
    indices = jnp.arange(SOURCES, dtype=jnp.int32)
    owner = indices // SRC_DEV
    live = indices % SRC_DEV < live_count[owner]
    live_mass = jnp.where(live, masses, jnp.float32(0.0))
    star = jnp.arange(NACT, dtype=jnp.int32) // ACT_DEV * SRC_DEV + active_slot
    state = jnp.concatenate([pos_pred[:, star], vel_pred[:, star], accel_old[:, star], jerk_old[:, star], elapsed[star][None]], axis=0)
    block_size = min(128, NACT)
    blocks = state[0:6].reshape(6, NACT // block_size, block_size).transpose(1, 0, 2)
    summed = lax.map(lambda blk: pair_terms(blk, pos_pred, vel_pred, live_mass), blocks)
    summed = summed.transpose(1, 0, 2).reshape(7, NACT)
    return correct(state, summed)
```

```python
import functools
import math

import jax
import jax.numpy as jnp
from jax import lax
from jax.experimental import pallas as pl
from jax.experimental.pallas import tpu as pltpu
from jax.sharding import PartitionSpec as P

MESH = pl.DeviceIdType.MESH
LANES = 128
TAU_BASE = 0.5
SOFTEN_SQ = 0.0001


def kernel(
    n_grp, n_dev, rows, batch,
    pos_ref, vel_ref, acc_ref, jerk_ref, mass_ref, level_ref, live_ref, slot_ref,
    pos_vel_ref, acc_jerk_ref, pot_ref,
    src, rest, act, total, send_sem, recv_sem,
):
    n = n_grp * n_dev
    n_src = pos_ref.shape[1]
    n_act = slot_ref.shape[1]
    me = lax.axis_index("grp") * n_dev + lax.axis_index("dev")

    def place(index):
        return (index // n_dev, lax.rem(index, n_dev))

    barrier = pltpu.get_barrier_semaphore()

    def greet(k, carry):
        pl.semaphore_signal(
            barrier, inc=1, device_id=place(lax.rem(me + k, n)), device_id_type=MESH
        )
        return carry

    lax.fori_loop(1, n, greet, 0)

    level = level_ref[...]
    step = jnp.full(level.shape, TAU_BASE, jnp.float32)
    step = jnp.where((level & 1) != 0, step * 0.5, step)
    step = jnp.where((level & 2) != 0, step * 0.25, step)
    step = jnp.where((level & 4) != 0, step * 0.0625, step)
    vel, acc, jerk = vel_ref[...], acc_ref[...], jerk_ref[...]
    pos_pred = pos_ref[...] + step * (vel + step * (acc * 0.5 + step * jerk * (1.0 / 6.0)))
    vel_pred = vel + step * (acc + step * jerk * 0.5)
    lane = lax.broadcasted_iota(jnp.int32, (1, n_src), 1)
    live_mass = jnp.where(lane < live_ref[0], mass_ref[...], 0.0)
    src[me, 0:3, :] = pos_pred
    src[me, 3:6, :] = vel_pred
    src[me, 6:7, :] = live_mass
    src[me, 7:8, :] = jnp.zeros_like(live_mass)
    rest[0:3, :] = acc
    rest[3:6, :] = jerk
    rest[6:7, :] = step
    rest[7:8, :] = jnp.zeros_like(step)

    pl.semaphore_wait(barrier, n - 1)

    def copy(index, other):
        return pltpu.make_async_remote_copy(
            src_ref=src.at[index],
            dst_ref=src.at[index],
            send_sem=send_sem.at[other],
            recv_sem=recv_sem.at[index],
            device_id=place(other),
            device_id_type=MESH,
        )

    def send(k, carry):
        copy(me, lax.rem(me + k, n)).start()
        return carry

    lax.fori_loop(1, n, send, 0)

    slot = jnp.broadcast_to(slot_ref[...], (8, n_act))
    low, part = slot & (LANES - 1), slot // LANES

    def pick(table):
        out = jnp.zeros((8, n_act), jnp.float32)
        for chunk in range(n_src // LANES):
            found = jnp.take_along_axis(table[:, chunk * LANES : (chunk + 1) * LANES], low, axis=1)
            out = jnp.where(part == chunk, found, out)
        return out

    state = pick(src[me])
    old = pick(rest[...])
    for c in range(6):
        act[c] = jnp.broadcast_to(state[c : c + 1], (LANES, n_act)).T
    total[...] = jnp.zeros_like(total)

    def sweep(turn, carry):
        blocks = []
        for b in range(batch):
            k = turn * batch + b
            index = lax.rem(me - k + n, n)
            blocks.append(index)

            @pl.when(k > 0)
            def _():
                copy(index, index).wait_recv()

        def group(g, carry):
            at = pl.ds(pl.multiple_of(g * rows, rows), rows)
            x, y, z, vx, vy, vz = [act[c, at, :] for c in range(6)]
            ax, ay, az, jx, jy, jz, pot = [total[c, at, :] for c in range(7)]
            for index in blocks:
                for chunk in range(n_src // LANES):
                    sx, sy, sz, svx, svy, svz, mass = [
                        src[index, c : c + 1, chunk * LANES : (chunk + 1) * LANES] for c in range(7)
                    ]
                    dx, dy, dz = sx - x, sy - y, sz - z
                    ex, ey, ez = svx - vx, svy - vy, svz - vz
                    inv = lax.rsqrt(dx * dx + dy * dy + dz * dz + SOFTEN_SQ)
                    inv_sq = inv * inv
                    w = mass * inv
                    u = w * inv_sq
                    radial = (3.0 * inv_sq) * (dx * ex + dy * ey + dz * ez)
                    px, py, pz = u * dx, u * dy, u * dz
                    ax, ay, az = ax + px, ay + py, az + pz
                    jx = jx + (u * ex - radial * px)
                    jy = jy + (u * ey - radial * py)
                    jz = jz + (u * ez - radial * pz)
                    pot = pot + w
            for c, value in enumerate((ax, ay, az, jx, jy, jz, pot)):
                total[c, at, :] = value
            return carry

        lax.fori_loop(0, n_act // rows, group, 0)
        return carry

    lax.fori_loop(0, n // batch, sweep, 0)

    for c in range(6):
        acc_jerk_ref[c : c + 1, :] = jnp.sum(total[c].T, axis=0, keepdims=True)
    pot_ref[...] = -jnp.sum(total[6].T, axis=0, keepdims=True)

    acc_end, jerk_end = acc_jerk_ref[0:3, :], acc_jerk_ref[3:6, :]
    acc_start, jerk_start, h = old[0:3], old[3:6], old[6:7]
    differ = acc_start - acc_end
    fourth = -6.0 * differ - h * (4.0 * jerk_start + 2.0 * jerk_end)
    fifth = 12.0 * differ + 6.0 * h * (jerk_start + jerk_end)
    pos_vel_ref[0:3, :] = state[0:3] + h * h * (1.0 / 24.0) * fourth + h * h * (1.0 / 120.0) * fifth
    pos_vel_ref[3:6, :] = state[3:6] + h * (1.0 / 6.0) * fourth + h * (1.0 / 24.0) * fifth

    def settle(k, carry):
        copy(me, lax.rem(me + k, n)).wait_send()
        return carry

    lax.fori_loop(1, n, settle, 0)


def solution(mesh):
    n_grp, n_dev = mesh.shape["grp"], mesh.shape["dev"]
    n = n_grp * n_dev

    def shards(positions, velocities, accel_old, jerk_old, masses, levels, live_count, active_slot):
        n_src, n_act = positions.shape[1], active_slot.shape[0]
        rows = math.gcd(16, n_act)
        batch = math.gcd(4, n)
        vmem = pl.BlockSpec(memory_space=pltpu.VMEM)
        pos_vel, acc_jerk, pot = pl.pallas_call(
            functools.partial(kernel, n_grp, n_dev, rows, batch),
            out_shape=(
                jax.ShapeDtypeStruct((6, n_act), jnp.float32),
                jax.ShapeDtypeStruct((6, n_act), jnp.float32),
                jax.ShapeDtypeStruct((1, n_act), jnp.float32),
            ),
            in_specs=[vmem] * 6 + [pl.BlockSpec(memory_space=pltpu.SMEM), vmem],
            out_specs=(vmem, vmem, vmem),
            scratch_shapes=[
                pltpu.VMEM((n, 8, n_src), jnp.float32),
                pltpu.VMEM((8, n_src), jnp.float32),
                pltpu.VMEM((6, n_act, LANES), jnp.float32),
                pltpu.VMEM((7, n_act, LANES), jnp.float32),
                pltpu.SemaphoreType.DMA((n,)),
                pltpu.SemaphoreType.DMA((n,)),
            ],
            compiler_params=pltpu.CompilerParams(
                collective_id=0, has_side_effects=True, vmem_limit_bytes=32 * 1024 * 1024
            ),
        )(
            positions, velocities, accel_old, jerk_old,
            masses[None], levels[None], live_count, active_slot[None],
        )
        return pos_vel, acc_jerk, pot[0]

    split = P(None, ("grp", "dev"))
    flat = P(("grp", "dev"))
    return jax.shard_map(
        shards,
        mesh=mesh,
        in_specs=(split, split, split, split, flat, flat, flat, flat),
        out_specs=(split, split, flat),
        check_vma=False,
    )
```

```python
import functools
import math

import jax
import jax.numpy as jnp
from jax import lax
from jax.experimental import pallas as pl
from jax.experimental.pallas import tpu as pltpu
from jax.sharding import PartitionSpec as P

MESH = pl.DeviceIdType.MESH
LANES = 128
TAU_BASE = 0.5
SOFTEN_SQ = 0.0001


def add_pairs(state, sums, source):
    x, y, z, vx, vy, vz = state
    ax, ay, az, jx, jy, jz, pot = sums
    sx, sy, sz, svx, svy, svz, mass = source
    dx, dy, dz = sx - x, sy - y, sz - z
    ex, ey, ez = svx - vx, svy - vy, svz - vz
    inv = lax.rsqrt(dx * dx + dy * dy + dz * dz + SOFTEN_SQ)
    inv_sq = inv * inv
    w = mass * inv
    u = w * inv_sq
    radial = (3.0 * inv_sq) * (dx * ex + dy * ey + dz * ez)
    px, py, pz = u * dx, u * dy, u * dz
    return (
        ax + px, ay + py, az + pz,
        jx + (u * ex - radial * px), jy + (u * ey - radial * py), jz + (u * ez - radial * pz),
        pot + w,
    )


def sweep(act, total, rows, chunks):
    def group(g, carry):
        at = pl.ds(pl.multiple_of(g * rows, rows), rows)
        state = [act[c, at, :] for c in range(6)]
        sums = tuple(total[c, at, :] for c in range(7))
        for chunk in chunks:
            sums = add_pairs(state, sums, [chunk(c) for c in range(7)])
        for c in range(7):
            total[c, at, :] = sums[c]
        return carry

    lax.fori_loop(0, act.shape[1] // rows, group, 0)


def share(
    n_grp, n_dev, rows, batch,
    pos_hbm, vel_hbm, acc_hbm, jerk_hbm, mass_hbm, level_hbm, live_hbm, slot_hbm,
    src, act, total, own,
    pos_ref, vel_ref, acc_ref, jerk_ref, mass_ref, level_ref, live_ref, slot_ref,
    rest, load_sem, send_sem, recv_sem,
):
    n = n_grp * n_dev
    n_src = pos_ref.shape[1]
    n_act = slot_ref.shape[1]
    n_chunk = n_src // LANES
    me = lax.axis_index("grp") * n_dev + lax.axis_index("dev")

    loads = [
        pltpu.make_async_copy(there, here, load_sem.at[i])
        for i, (there, here) in enumerate((
            (pos_hbm, pos_ref), (vel_hbm, vel_ref), (acc_hbm, acc_ref), (jerk_hbm, jerk_ref),
            (mass_hbm, mass_ref), (level_hbm, level_ref), (live_hbm, live_ref), (slot_hbm, slot_ref),
        ))
    ]
    for load in loads:
        load.start()

    def place(index):
        return (index // n_dev, lax.rem(index, n_dev))

    barrier = pltpu.get_barrier_semaphore()

    def greet(k, carry):
        pl.semaphore_signal(
            barrier, inc=1, device_id=place(lax.rem(me + k, n)), device_id_type=MESH
        )
        return carry

    lax.fori_loop(1, n, greet, 0)
    total[...] = jnp.zeros_like(total)
    for load in loads:
        load.wait()

    level = level_ref[...]
    step = jnp.full(level.shape, TAU_BASE, jnp.float32)
    step = jnp.where((level & 1) != 0, step * 0.5, step)
    step = jnp.where((level & 2) != 0, step * 0.25, step)
    step = jnp.where((level & 4) != 0, step * 0.0625, step)
    vel, acc, jerk = vel_ref[...], acc_ref[...], jerk_ref[...]
    pos_pred = pos_ref[...] + step * (vel + step * (acc * 0.5 + step * jerk * (1.0 / 6.0)))
    vel_pred = vel + step * (acc + step * jerk * 0.5)
    lane = lax.broadcasted_iota(jnp.int32, (1, n_src), 1)
    live = jnp.full((1, n_src), live_ref[0], jnp.int32)
    live_mass = jnp.where(lane < live, mass_ref[...], 0.0)
    count = live.astype(jnp.float32)
    for chunk in range(n_chunk):
        cut = slice(chunk * LANES, (chunk + 1) * LANES)
        src[me, chunk, 0:3, :] = pos_pred[:, cut]
        src[me, chunk, 3:6, :] = vel_pred[:, cut]
        src[me, chunk, 6:7, :] = live_mass[:, cut]
        src[me, chunk, 7:8, :] = count[:, cut]
    rest[0:3, :] = acc
    rest[3:6, :] = jerk
    rest[6:7, :] = step
    rest[7:8, :] = jnp.zeros_like(step)

    pl.semaphore_wait(barrier, n - 1)

    def copy(index, other):
        return pltpu.make_async_remote_copy(
            src_ref=src.at[index],
            dst_ref=src.at[index],
            send_sem=send_sem.at[other],
            recv_sem=recv_sem.at[index],
            device_id=place(other),
            device_id_type=MESH,
        )

    def send(k, carry):
        copy(me, lax.rem(me + k, n)).start()
        return carry

    lax.fori_loop(1, n, send, 0)

    slot = jnp.broadcast_to(slot_ref[...], (8, n_act))
    low, part = slot & (LANES - 1), slot // LANES

    def pick(chunk_of):
        out = jnp.zeros((8, n_act), jnp.float32)
        for chunk in range(n_chunk):
            found = jnp.take_along_axis(chunk_of(chunk), low, axis=1)
            out = jnp.where(part == chunk, found, out)
        return out

    state = pick(lambda chunk: src[me, chunk])
    own[0:8, :] = state
    own[8:16, :] = pick(lambda chunk: rest[:, chunk * LANES : (chunk + 1) * LANES])
    for c in range(6):
        act[c] = jnp.broadcast_to(state[c : c + 1], (LANES, n_act)).T

    def arrive(turn, carry):
        chunks = []
        for b in range(batch):
            k = turn * batch + b
            index = lax.rem(me - k + n, n)
            chunks.append(lambda c, index=index: src[index, 0, c : c + 1, :])

            @pl.when(k > 0)
            def _():
                copy(index, index).wait_recv()

        sweep(act, total, rows, chunks)
        return carry

    lax.fori_loop(0, n // batch, arrive, 0)

    def settle(k, carry):
        copy(me, lax.rem(me + k, n)).wait_send()
        return carry

    lax.fori_loop(1, n, settle, 0)


def finish(
    rows, batch,
    src, act, total, own,
    pos_vel_hbm, acc_jerk_hbm, pot_hbm,
    packed, more, pos_vel_ref, acc_jerk_ref, pot_ref, store_sem,
):
    n, n_chunk = src.shape[0], src.shape[1]
    lane = lax.broadcasted_iota(jnp.int32, (8, LANES), 1)
    row = lax.broadcasted_iota(jnp.int32, (8, LANES), 0)
    more[...] = jnp.zeros_like(more)

    unroll = math.gcd(8, n)

    def pack(turn, carry):
        filled, now = carry
        counts = [src[turn * unroll + b, 0, 7, 0].astype(jnp.int32) for b in range(unroll)]
        for b in range(unroll):
            for chunk in range(1, n_chunk):
                many = jnp.minimum(jnp.maximum(counts[b] - chunk * LANES, 0), LANES)
                start = lax.rem(filled, LANES)
                moved = pltpu.roll(src[turn * unroll + b, chunk], start, 1)
                now = jnp.where(lane >= start, moved, now)
                packed[filled // LANES] = now
                now = jnp.where(start + many >= LANES, moved, now)
                filled = filled + many
        return filled, now

    filled, now = lax.fori_loop(
        0, n // unroll, pack, (jnp.int32(0), jnp.zeros((8, LANES), jnp.float32))
    )
    last = filled // LANES
    packed[last] = jnp.where((row == 6) & (lane >= lax.rem(filled, LANES)), 0.0, now)
    for b in range(1, batch):
        packed[last + b] = jnp.zeros((8, LANES), jnp.float32)

    def turns(turn, carry):
        sweep(act, more, rows, [
            lambda c, at=turn * batch + b: packed[at, c : c + 1, :] for b in range(batch)
        ])
        return carry

    lax.fori_loop(0, (filled + batch * LANES - 1) // (batch * LANES), turns, 0)

    for c in range(6):
        acc_jerk_ref[c : c + 1, :] = jnp.sum((total[c] + more[c]).T, axis=0, keepdims=True)
    pot_ref[...] = -jnp.sum((total[6] + more[6]).T, axis=0, keepdims=True)
    stores = [
        pltpu.make_async_copy(here, there, store_sem.at[i])
        for i, (here, there) in enumerate((
            (acc_jerk_ref, acc_jerk_hbm), (pot_ref, pot_hbm), (pos_vel_ref, pos_vel_hbm),
        ))
    ]
    stores[0].start()
    stores[1].start()

    acc_end, jerk_end = acc_jerk_ref[0:3, :], acc_jerk_ref[3:6, :]
    pos_now, vel_now = own[0:3, :], own[3:6, :]
    acc_start, jerk_start, h = own[8:11, :], own[11:14, :], own[14:15, :]
    differ = acc_start - acc_end
    fourth = -6.0 * differ - h * (4.0 * jerk_start + 2.0 * jerk_end)
    fifth = 12.0 * differ + 6.0 * h * (jerk_start + jerk_end)
    pos_vel_ref[0:3, :] = pos_now + h * h * (1.0 / 24.0) * fourth + h * h * (1.0 / 120.0) * fifth
    pos_vel_ref[3:6, :] = vel_now + h * (1.0 / 6.0) * fourth + h * (1.0 / 24.0) * fifth
    stores[2].start()
    for store in stores:
        store.wait()


def solution(mesh):
    n_grp, n_dev = mesh.shape["grp"], mesh.shape["dev"]
    n = n_grp * n_dev

    def shards(positions, velocities, accel_old, jerk_old, masses, levels, live_count, active_slot):
        n_src, n_act = positions.shape[1], active_slot.shape[0]
        n_chunk = n_src // LANES
        vmem = pl.BlockSpec(memory_space=pltpu.VMEM)
        hbm = pl.BlockSpec(memory_space=pltpu.HBM)
        args = (
            positions, velocities, accel_old, jerk_old,
            masses[None], levels[None], live_count, active_slot[None],
        )
        f32 = jnp.float32
        middle = pl.pallas_call(
            functools.partial(share, n_grp, n_dev, math.gcd(16, n_act), math.gcd(4, n)),
            out_shape=(
                jax.ShapeDtypeStruct((n, n_chunk, 8, LANES), f32),
                jax.ShapeDtypeStruct((6, n_act, LANES), f32),
                jax.ShapeDtypeStruct((7, n_act, LANES), f32),
                jax.ShapeDtypeStruct((16, n_act), f32),
            ),
            in_specs=[hbm] * 8,
            out_specs=(vmem,) * 4,
            scratch_shapes=[
                (pltpu.SMEM if a is live_count else pltpu.VMEM)(a.shape, a.dtype) for a in args
            ] + [
                pltpu.VMEM((8, n_src), f32),
                pltpu.SemaphoreType.DMA((8,)),
                pltpu.SemaphoreType.DMA((n,)),
                pltpu.SemaphoreType.DMA((n,)),
            ],
            compiler_params=pltpu.CompilerParams(
                collective_id=0, has_side_effects=True, vmem_limit_bytes=60 * 1024 * 1024
            ),
        )(*args)
        batch = 2
        pos_vel, acc_jerk, pot = pl.pallas_call(
            functools.partial(finish, math.gcd(32, n_act), batch),
            out_shape=(
                jax.ShapeDtypeStruct((6, n_act), f32),
                jax.ShapeDtypeStruct((6, n_act), f32),
                jax.ShapeDtypeStruct((1, n_act), f32),
            ),
            in_specs=[vmem] * 4,
            out_specs=(hbm,) * 3,
            scratch_shapes=[
                pltpu.VMEM((n * (n_chunk - 1) + batch, 8, LANES), f32),
                pltpu.VMEM((7, n_act, LANES), f32),
                pltpu.VMEM((6, n_act), f32),
                pltpu.VMEM((6, n_act), f32),
                pltpu.VMEM((1, n_act), f32),
                pltpu.SemaphoreType.DMA((3,)),
            ],
            compiler_params=pltpu.CompilerParams(vmem_limit_bytes=60 * 1024 * 1024),
        )(*middle)
        return pos_vel, acc_jerk, pot[0]

    split = P(None, ("grp", "dev"))
    flat = P(("grp", "dev"))
    return jax.shard_map(
        shards,
        mesh=mesh,
        in_specs=(split, split, split, split, flat, flat, flat, flat),
        out_specs=(split, split, flat),
        check_vma=False,
    )
```

```python
import functools
import math

import jax
import jax.numpy as jnp
from jax import lax
from jax.experimental import pallas as pl
from jax.experimental.pallas import tpu as pltpu
from jax.sharding import PartitionSpec as P

MESH = pl.DeviceIdType.MESH
LANES = 128
TAU_BASE = 0.5
SOFTEN_SQ = 0.0001


def add_pairs(state, sums, source):
    x, y, z, vx, vy, vz = state
    ax, ay, az, jx, jy, jz, pot = sums
    sx, sy, sz, svx, svy, svz, mass = source
    dx, dy, dz = sx - x, sy - y, sz - z
    ex, ey, ez = svx - vx, svy - vy, svz - vz
    inv = lax.rsqrt(dx * dx + dy * dy + dz * dz + SOFTEN_SQ)
    inv_sq = inv * inv
    w = mass * inv
    u = w * inv_sq
    radial = (3.0 * inv_sq) * (dx * ex + dy * ey + dz * ez)
    px, py, pz = u * dx, u * dy, u * dz
    return (
        ax + px, ay + py, az + pz,
        jx + (u * ex - radial * px), jy + (u * ey - radial * py), jz + (u * ez - radial * pz),
        pot + w,
    )


def sweep(act, total, rows, chunks):
    def group(g, carry):
        at = pl.ds(pl.multiple_of(g * rows, rows), rows)
        state = [act[c, at, :] for c in range(6)]
        sums = tuple(total[c, at, :] for c in range(7))
        for chunk in chunks:
            sums = add_pairs(state, sums, [chunk(c) for c in range(7)])
        for c in range(7):
            total[c, at, :] = sums[c]
        return carry

    lax.fori_loop(0, act.shape[1] // rows, group, 0)


def spread(own, act):
    for c in range(6):
        act[c] = jnp.broadcast_to(own[c : c + 1, :], (LANES, own.shape[1])).T


def share(
    n_grp, n_line, n_core, rows, batch,
    pos_hbm, vel_hbm, acc_hbm, jerk_hbm, mass_hbm, level_hbm, live_hbm, slot_hbm,
    beyond_hbm, total_hbm, own_hbm,
    pos_ref, vel_ref, acc_ref, jerk_ref, mass_ref, level_ref, live_ref, slot_ref,
    src, act, total, own, rest,
    load_sem, line_send, line_recv, grp_send, grp_recv, core_send, core_recv, beyond_sem, out_sem,
):
    n_src = pos_ref.shape[1]
    n_act = slot_ref.shape[1]
    n_chunk = n_src // LANES
    grp = lax.axis_index("grp")
    dev = lax.axis_index("dev")
    line, core = dev // n_core, lax.rem(dev, n_core)
    twin = n_core - 1 - core

    loads = [
        pltpu.make_async_copy(there, here, load_sem.at[i])
        for i, (there, here) in enumerate((
            (pos_hbm, pos_ref), (vel_hbm, vel_ref), (acc_hbm, acc_ref), (jerk_hbm, jerk_ref),
            (mass_hbm, mass_ref), (level_hbm, level_ref), (live_hbm, live_ref), (slot_hbm, slot_ref),
        ))
    ]
    for load in loads:
        load.start()

    def on_line(k):
        return lax.rem(line + k, n_line)

    def on_grp(k):
        return lax.rem(grp + k, n_grp)

    def each(count, body):
        def one(k, carry):
            body(k)
            return carry

        lax.fori_loop(1, count, one, 0)

    barrier = pltpu.get_barrier_semaphore()

    def greet(place):
        pl.semaphore_signal(barrier, inc=1, device_id=place, device_id_type=MESH)

    each(n_line, lambda k: greet((grp, on_line(k) * n_core + core)))
    each(n_grp, lambda k: greet((on_grp(k), dev)))
    if n_core > 1:
        greet((grp, line * n_core + twin))
    total[...] = jnp.zeros_like(total)
    for load in loads:
        load.wait()

    mine = src.at[core, grp, line]
    level = level_ref[...]
    step = jnp.full(level.shape, TAU_BASE, jnp.float32)
    step = jnp.where((level & 1) != 0, step * 0.5, step)
    step = jnp.where((level & 2) != 0, step * 0.25, step)
    step = jnp.where((level & 4) != 0, step * 0.0625, step)
    vel, acc, jerk = vel_ref[...], acc_ref[...], jerk_ref[...]
    pos_pred = pos_ref[...] + step * (vel + step * (acc * 0.5 + step * jerk * (1.0 / 6.0)))
    vel_pred = vel + step * (acc + step * jerk * 0.5)
    lane = lax.broadcasted_iota(jnp.int32, (1, n_src), 1)
    live = jnp.full((1, n_src), live_ref[0], jnp.int32)
    live_mass = jnp.where(lane < live, mass_ref[...], 0.0)
    count = live.astype(jnp.float32)
    for chunk in range(n_chunk):
        cut = slice(chunk * LANES, (chunk + 1) * LANES)
        mine[chunk, 0:3, :] = pos_pred[:, cut]
        mine[chunk, 3:6, :] = vel_pred[:, cut]
        mine[chunk, 6:7, :] = live_mass[:, cut]
        mine[chunk, 7:8, :] = count[:, cut]
    rest[0:3, :] = acc
    rest[3:6, :] = jerk
    rest[6:7, :] = step
    rest[7:8, :] = jnp.zeros_like(step)

    pl.semaphore_wait(barrier, (n_line - 1) + (n_grp - 1) + (n_core - 1))

    def line_copy(origin, other):
        block = src.at[core, grp, origin]
        return pltpu.make_async_remote_copy(
            src_ref=block, dst_ref=block,
            send_sem=line_send.at[other], recv_sem=line_recv.at[origin],
            device_id=(grp, other * n_core + core), device_id_type=MESH,
        )

    def grp_copy(origin, other):
        block = src.at[core, origin]
        return pltpu.make_async_remote_copy(
            src_ref=block, dst_ref=block,
            send_sem=grp_send.at[other], recv_sem=grp_recv.at[origin],
            device_id=(other, dev), device_id_type=MESH,
        )

    def core_copy(owner, origin):
        block = src.at[owner, origin]
        return pltpu.make_async_remote_copy(
            src_ref=block, dst_ref=block,
            send_sem=core_send.at[origin], recv_sem=core_recv.at[origin],
            device_id=(grp, line * n_core + twin), device_id_type=MESH,
        )

    def keep(owner, origin):
        return pltpu.make_async_copy(
            src.at[owner, origin, :, 1:], beyond_hbm.at[owner, origin], beyond_sem.at[owner, origin]
        )

    def add(owner, origin):
        def turn(t, carry):
            sweep(act, total, rows, [
                lambda c, at=t * batch + b: src[owner, origin, at, 0, c : c + 1, :]
                for b in range(batch)
            ])
            return carry

        lax.fori_loop(0, n_line // batch, turn, 0)

    each(n_line, lambda k: line_copy(line, on_line(k)).start())

    slot = jnp.broadcast_to(slot_ref[...], (8, n_act))
    low, part = slot & (LANES - 1), slot // LANES

    def pick(chunk_of):
        out = jnp.zeros((8, n_act), jnp.float32)
        for chunk in range(n_chunk):
            found = jnp.take_along_axis(chunk_of(chunk), low, axis=1)
            out = jnp.where(part == chunk, found, out)
        return out

    state = pick(lambda chunk: mine[chunk])
    own[0:8, :] = state
    own[8:16, :] = pick(lambda chunk: rest[:, chunk * LANES : (chunk + 1) * LANES])
    own_copy = pltpu.make_async_copy(own, own_hbm, out_sem.at[0])
    own_copy.start()
    spread(own, act)

    each(n_line, lambda k: line_copy(on_line(k), on_line(k)).wait_recv())
    each(n_grp, lambda k: grp_copy(grp, on_grp(k)).start())
    if n_core > 1:
        core_copy(core, grp).start()
    keep(core, grp).start()
    add(core, grp)
    if n_core > 1:
        core_copy(twin, grp).wait_recv()
        keep(twin, grp).start()
        add(twin, grp)

    def forward(k):
        origin = on_grp(k)
        grp_copy(origin, origin).wait_recv()
        if n_core > 1:
            core_copy(core, origin).start()
        keep(core, origin).start()

    each(n_grp, forward)
    each(n_grp, lambda k: add(core, on_grp(k)))

    if n_core > 1:
        def last(k):
            origin = on_grp(k)
            core_copy(twin, origin).wait_recv()
            keep(twin, origin).start()
            add(twin, origin)

        each(n_grp, last)

    total_copy = pltpu.make_async_copy(total, total_hbm, out_sem.at[1])
    total_copy.start()
    each(n_line, lambda k: line_copy(line, on_line(k)).wait_send())
    each(n_grp, lambda k: grp_copy(grp, on_grp(k)).wait_send())

    def settle(origin, carry):
        if n_core > 1:
            core_copy(core, origin).wait_send()
        for owner in range(n_core):
            keep(owner, origin).wait()
        return carry

    lax.fori_loop(0, n_grp, settle, 0)
    own_copy.wait()
    total_copy.wait()


def finish(
    rows, batch,
    beyond_hbm, total_hbm, own_hbm,
    pos_vel_hbm, acc_jerk_hbm, pot_hbm,
    beyond, total, own, act, packed, more, pos_vel_ref, acc_jerk_ref, pot_ref, load_sem, store_sem,
):
    n, n_beyond = beyond.shape[0], beyond.shape[1]
    loads = [
        pltpu.make_async_copy(there, here, load_sem.at[i])
        for i, (there, here) in enumerate(((own_hbm, own), (beyond_hbm, beyond), (total_hbm, total)))
    ]
    for load in loads:
        load.start()
    lane = lax.broadcasted_iota(jnp.int32, (8, LANES), 1)
    row = lax.broadcasted_iota(jnp.int32, (8, LANES), 0)
    more[...] = jnp.zeros_like(more)
    loads[0].wait()
    spread(own, act)
    loads[1].wait()

    unroll = math.gcd(8, n)

    def pack(turn, carry):
        filled, now = carry
        counts = [beyond[turn * unroll + b, 0, 7, 0].astype(jnp.int32) for b in range(unroll)]
        for b in range(unroll):
            for chunk in range(n_beyond):
                many = jnp.minimum(jnp.maximum(counts[b] - (chunk + 1) * LANES, 0), LANES)
                start = lax.rem(filled, LANES)
                moved = pltpu.roll(beyond[turn * unroll + b, chunk], start, 1)
                now = jnp.where(lane >= start, moved, now)
                packed[filled // LANES] = now
                now = jnp.where(start + many >= LANES, moved, now)
                filled = filled + many
        return filled, now

    filled, now = lax.fori_loop(
        0, n // unroll, pack, (jnp.int32(0), jnp.zeros((8, LANES), jnp.float32))
    )
    last = filled // LANES
    packed[last] = jnp.where((row == 6) & (lane >= lax.rem(filled, LANES)), 0.0, now)
    for b in range(1, batch):
        packed[last + b] = jnp.zeros((8, LANES), jnp.float32)

    def turns(turn, carry):
        sweep(act, more, rows, [
            lambda c, at=turn * batch + b: packed[at, c : c + 1, :] for b in range(batch)
        ])
        return carry

    lax.fori_loop(0, (filled + batch * LANES - 1) // (batch * LANES), turns, 0)

    loads[2].wait()
    for c in range(6):
        acc_jerk_ref[c : c + 1, :] = jnp.sum((total[c] + more[c]).T, axis=0, keepdims=True)
    pot_ref[...] = -jnp.sum((total[6] + more[6]).T, axis=0, keepdims=True)
    stores = [
        pltpu.make_async_copy(here, there, store_sem.at[i])
        for i, (here, there) in enumerate((
            (acc_jerk_ref, acc_jerk_hbm), (pot_ref, pot_hbm), (pos_vel_ref, pos_vel_hbm),
        ))
    ]
    stores[0].start()
    stores[1].start()

    acc_end, jerk_end = acc_jerk_ref[0:3, :], acc_jerk_ref[3:6, :]
    pos_now, vel_now = own[0:3, :], own[3:6, :]
    acc_start, jerk_start, h = own[8:11, :], own[11:14, :], own[14:15, :]
    differ = acc_start - acc_end
    fourth = -6.0 * differ - h * (4.0 * jerk_start + 2.0 * jerk_end)
    fifth = 12.0 * differ + 6.0 * h * (jerk_start + jerk_end)
    pos_vel_ref[0:3, :] = pos_now + h * h * (1.0 / 24.0) * fourth + h * h * (1.0 / 120.0) * fifth
    pos_vel_ref[3:6, :] = vel_now + h * (1.0 / 6.0) * fourth + h * (1.0 / 24.0) * fifth
    stores[2].start()
    for store in stores:
        store.wait()


def solution(mesh):
    n_grp, n_dev = mesh.shape["grp"], mesh.shape["dev"]
    n = n_grp * n_dev

    def shards(positions, velocities, accel_old, jerk_old, masses, levels, live_count, active_slot):
        n_src, n_act = positions.shape[1], active_slot.shape[0]
        n_chunk = n_src // LANES
        hbm = pl.BlockSpec(memory_space=pltpu.HBM)
        args = (
            positions, velocities, accel_old, jerk_old,
            masses[None], levels[None], live_count, active_slot[None],
        )
        f32 = jnp.float32
        n_core = math.gcd(2, n_dev)
        n_line = n_dev // n_core
        dma = pltpu.SemaphoreType.DMA
        beyond, total, own = pl.pallas_call(
            functools.partial(
                share, n_grp, n_line, n_core, math.gcd(16, n_act), math.gcd(4, n_line)
            ),
            out_shape=(
                jax.ShapeDtypeStruct((n_core, n_grp, n_line, n_chunk - 1, 8, LANES), f32),
                jax.ShapeDtypeStruct((7, n_act, LANES), f32),
                jax.ShapeDtypeStruct((16, n_act), f32),
            ),
            in_specs=[hbm] * 8,
            out_specs=(hbm,) * 3,
            scratch_shapes=[
                (pltpu.SMEM if a is live_count else pltpu.VMEM)(a.shape, a.dtype) for a in args
            ] + [
                pltpu.VMEM((n_core, n_grp, n_line, n_chunk, 8, LANES), f32),
                pltpu.VMEM((6, n_act, LANES), f32),
                pltpu.VMEM((7, n_act, LANES), f32),
                pltpu.VMEM((16, n_act), f32),
                pltpu.VMEM((8, n_src), f32),
                dma((8,)),
                dma((n_line,)), dma((n_line,)),
                dma((n_grp,)), dma((n_grp,)),
                dma((n_grp,)), dma((n_grp,)),
                dma((n_core, n_grp)),
                dma((2,)),
            ],
            compiler_params=pltpu.CompilerParams(
                collective_id=0, has_side_effects=True, vmem_limit_bytes=60 * 1024 * 1024
            ),
        )(*args)
        batch = 2
        pos_vel, acc_jerk, pot = pl.pallas_call(
            functools.partial(finish, math.gcd(32, n_act), batch),
            out_shape=(
                jax.ShapeDtypeStruct((6, n_act), f32),
                jax.ShapeDtypeStruct((6, n_act), f32),
                jax.ShapeDtypeStruct((1, n_act), f32),
            ),
            in_specs=[hbm] * 3,
            out_specs=(hbm,) * 3,
            scratch_shapes=[
                pltpu.VMEM((n, n_chunk - 1, 8, LANES), f32),
                pltpu.VMEM((7, n_act, LANES), f32),
                pltpu.VMEM((16, n_act), f32),
                pltpu.VMEM((6, n_act, LANES), f32),
                pltpu.VMEM((n * (n_chunk - 1) + batch, 8, LANES), f32),
                pltpu.VMEM((7, n_act, LANES), f32),
                pltpu.VMEM((6, n_act), f32),
                pltpu.VMEM((6, n_act), f32),
                pltpu.VMEM((1, n_act), f32),
                dma((3,)),
                dma((3,)),
            ],
            compiler_params=pltpu.CompilerParams(vmem_limit_bytes=60 * 1024 * 1024),
        )(beyond.reshape(n, n_chunk - 1, 8, LANES), total, own)
        return pos_vel, acc_jerk, pot[0]

    split = P(None, ("grp", "dev"))
    flat = P(("grp", "dev"))
    return jax.shard_map(
        shards,
        mesh=mesh,
        in_specs=(split, split, split, split, flat, flat, flat, flat),
        out_specs=(split, split, flat),
        check_vma=False,
    )
```

```python
import functools
import math

import jax
import jax.numpy as jnp
from jax import lax
from jax.experimental import pallas as pl
from jax.experimental.pallas import tpu as pltpu
from jax.sharding import PartitionSpec as P

MESH = pl.DeviceIdType.MESH
LANES = 128
TAU_BASE = 0.5
SOFTEN_SQ = 0.0001


def add_pairs(state, sums, source):
    x, y, z, vx, vy, vz = state
    ax, ay, az, jx, jy, jz, pot = sums
    sx, sy, sz, svx, svy, svz, mass = source
    dx, dy, dz = sx - x, sy - y, sz - z
    ex, ey, ez = svx - vx, svy - vy, svz - vz
    inv = lax.rsqrt(dx * dx + dy * dy + dz * dz + SOFTEN_SQ)
    inv_sq = inv * inv
    w = mass * inv
    u = w * inv_sq
    radial = (3.0 * inv_sq) * (dx * ex + dy * ey + dz * ez)
    px, py, pz = u * dx, u * dy, u * dz
    return (
        ax + px, ay + py, az + pz,
        jx + (u * ex - radial * px), jy + (u * ey - radial * py), jz + (u * ez - radial * pz),
        pot + w,
    )


def sweep(act, total, rows, fresh, chunks):
    def group(g, carry):
        at = pl.ds(pl.multiple_of(g * rows, rows), rows)
        state = [act[c, at, :] for c in range(6)]
        if fresh:
            sums = (jnp.zeros((rows, LANES), jnp.float32),) * 7
        else:
            sums = tuple(total[c, at, :] for c in range(7))
        for chunk in chunks:
            sums = add_pairs(state, sums, [chunk(c) for c in range(7)])
        for c in range(7):
            total[c, at, :] = sums[c]
        return carry

    lax.fori_loop(0, act.shape[1] // rows, group, 0)


def share(
    n_grp, n_dev, few, many,
    pos_hbm, vel_hbm, acc_hbm, jerk_hbm, mass_hbm, level_hbm, live_hbm, slot_hbm,
    out_hbm,
    pos_ref, vel_ref, acc_ref, jerk_ref, mass_ref, level_ref, live_ref, slot_ref,
    src, stars, act, total, rest, part, gain, out,
    load_sem, src_send, src_recv, star_send, star_recv, part_send, part_recv, out_sem,
):
    n_src = pos_ref.shape[1]
    n_act = slot_ref.shape[1]
    n_chunk = n_src // LANES
    grp, dev = lax.axis_index("grp"), lax.axis_index("dev")

    loads = [
        pltpu.make_async_copy(there, here, load_sem.at[i])
        for i, (there, here) in enumerate((
            (pos_hbm, pos_ref), (vel_hbm, vel_ref), (acc_hbm, acc_ref), (jerk_hbm, jerk_ref),
            (mass_hbm, mass_ref), (level_hbm, level_ref), (live_hbm, live_ref), (slot_hbm, slot_ref),
        ))
    ]
    for load in loads:
        load.start()

    def on_dev(k):
        return lax.rem(dev + k, n_dev)

    def on_grp(k):
        return lax.rem(grp + k, n_grp)

    def each(count, body):
        def one(k, carry):
            body(k)
            return carry

        lax.fori_loop(1, count, one, 0)

    barrier = pltpu.get_barrier_semaphore()

    def greet(place):
        pl.semaphore_signal(barrier, inc=1, device_id=place, device_id_type=MESH)

    each(n_dev, lambda k: greet((grp, on_dev(k))))
    each(n_grp, lambda k: greet((on_grp(k), dev)))
    for load in loads:
        load.wait()

    mine = src.at[dev]
    level = level_ref[...]
    step = jnp.full(level.shape, TAU_BASE, jnp.float32)
    step = jnp.where((level & 1) != 0, step * 0.5, step)
    step = jnp.where((level & 2) != 0, step * 0.25, step)
    step = jnp.where((level & 4) != 0, step * 0.0625, step)
    vel, acc, jerk = vel_ref[...], acc_ref[...], jerk_ref[...]
    pos_pred = pos_ref[...] + step * (vel + step * (acc * 0.5 + step * jerk * (1.0 / 6.0)))
    vel_pred = vel + step * (acc + step * jerk * 0.5)
    lane = lax.broadcasted_iota(jnp.int32, (1, n_src), 1)
    live_mass = jnp.where(lane < live_ref[0], mass_ref[...], 0.0)
    blank = jnp.zeros_like(step)
    for chunk in range(n_chunk):
        cut = slice(chunk * LANES, (chunk + 1) * LANES)
        mine[chunk, 0:3, :] = pos_pred[:, cut]
        mine[chunk, 3:6, :] = vel_pred[:, cut]
        mine[chunk, 6:7, :] = live_mass[:, cut]
        mine[chunk, 7:8, :] = blank[:, cut]
    rest[0:3, :] = acc
    rest[3:6, :] = jerk
    rest[6:7, :] = step
    rest[7:8, :] = blank

    pl.semaphore_wait(barrier, (n_dev - 1) + (n_grp - 1))

    def src_copy(origin, other):
        return pltpu.make_async_remote_copy(
            src_ref=src.at[origin], dst_ref=src.at[origin],
            send_sem=src_send.at[other], recv_sem=src_recv.at[origin],
            device_id=(grp, other), device_id_type=MESH,
        )

    def star_copy(origin, other):
        return pltpu.make_async_remote_copy(
            src_ref=stars.at[origin], dst_ref=stars.at[origin],
            send_sem=star_send.at[other], recv_sem=star_recv.at[origin],
            device_id=(other, dev), device_id_type=MESH,
        )

    def part_copy(origin, other):
        return pltpu.make_async_remote_copy(
            src_ref=part.at[other], dst_ref=gain.at[origin],
            send_sem=part_send.at[other], recv_sem=part_recv.at[origin],
            device_id=(other, dev), device_id_type=MESH,
        )

    each(n_dev, lambda k: src_copy(dev, on_dev(k)).start())

    slot = jnp.broadcast_to(slot_ref[...], (8, n_act))
    low, place = slot & (LANES - 1), slot // LANES

    def pick(chunk_of):
        found = jnp.zeros((8, n_act), jnp.float32)
        for chunk in range(n_chunk):
            here = jnp.take_along_axis(chunk_of(chunk), low, axis=1)
            found = jnp.where(place == chunk, here, found)
        return found

    state = pick(lambda chunk: mine[chunk])
    stars[grp] = state
    each(n_grp, lambda k: star_copy(grp, on_grp(k)).start())
    old = pick(lambda chunk: rest[:, chunk * LANES : (chunk + 1) * LANES])

    def spread(origin):
        for c in range(6):
            act[origin, c] = jnp.broadcast_to(stars[origin, c : c + 1, :], (LANES, n_act)).T

    spread(grp)

    def meet(k):
        origin = on_grp(k)
        star_copy(origin, origin).wait_recv()
        spread(origin)

    each(n_grp, meet)

    def add(origin, batch, turn, fresh, arriving):
        chunks = []
        for b in range(batch):
            k = turn * batch + b
            index = on_dev(k)
            chunks += [
                lambda c, index=index, chunk=chunk: src[index, chunk, c : c + 1, :]
                for chunk in range(n_chunk)
            ]
            if arriving and not (fresh and b == 0):
                src_copy(index, index).wait_recv()
        sweep(act.at[origin], total, math.gcd(16, n_act), fresh, chunks)

    def add_all(origin, batch, arriving):
        add(origin, batch, 0, True, arriving)

        def turns(turn, carry):
            add(origin, batch, turn, False, arriving)
            return carry

        lax.fori_loop(1, n_dev // batch, turns, 0)

    def total_of(c):
        return jnp.sum(total[c].T, axis=0, keepdims=True)

    def give(k, batch, arriving):
        origin = on_grp(k)
        add_all(origin, batch, arriving)
        for c in range(7):
            part[origin, c : c + 1, :] = total_of(c)
        part[origin, 7:8, :] = jnp.zeros((1, n_act), jnp.float32)
        part_copy(grp, origin).start()

    if n_grp > 1:
        give(1, few, True)

    def give_next(k, carry):
        give(k, many, False)
        return carry

    lax.fori_loop(2, n_grp, give_next, 0)
    add_all(grp, many, n_grp == 1)
    for c in range(7):
        part[grp, c : c + 1, :] = total_of(c)
    part[grp, 7:8, :] = jnp.zeros((1, n_act), jnp.float32)

    def gather(k, summed):
        origin = on_grp(k)
        part_copy(origin, origin).wait_recv()
        return summed + gain[origin]

    summed = lax.fori_loop(1, n_grp, gather, part[grp])

    acc_end, jerk_end = summed[0:3], summed[3:6]
    acc_start, jerk_start, h = old[0:3], old[3:6], old[6:7]
    differ = acc_start - acc_end
    fourth = -6.0 * differ - h * (4.0 * jerk_start + 2.0 * jerk_end)
    fifth = 12.0 * differ + 6.0 * h * (jerk_start + jerk_end)
    out[0, 0:3, :] = state[0:3] + h * h * (1.0 / 24.0) * fourth + h * h * (1.0 / 120.0) * fifth
    out[0, 3:6, :] = state[3:6] + h * (1.0 / 6.0) * fourth + h * (1.0 / 24.0) * fifth
    out[0, 6:8, :] = jnp.zeros((2, n_act), jnp.float32)
    out[1] = summed
    out[2] = jnp.broadcast_to(-summed[6:7], (8, n_act))
    out_copy = pltpu.make_async_copy(out, out_hbm, out_sem)
    out_copy.start()
    each(n_dev, lambda k: src_copy(dev, on_dev(k)).wait_send())
    each(n_grp, lambda k: star_copy(grp, on_grp(k)).wait_send())
    each(n_grp, lambda k: part_copy(grp, on_grp(k)).wait_send())
    out_copy.wait()


def hand_out(all_hbm, pos_vel_hbm, acc_jerk_hbm, pot_hbm, sem):
    copies = [
        pltpu.make_async_copy(all_hbm.at[0, 0:6], pos_vel_hbm, sem.at[0]),
        pltpu.make_async_copy(all_hbm.at[1, 0:6], acc_jerk_hbm, sem.at[1]),
        pltpu.make_async_copy(all_hbm.at[2, 0:1], pot_hbm, sem.at[2]),
    ]
    for copy in copies:
        copy.start()
    for copy in copies:
        copy.wait()


def solution(mesh):
    n_grp, n_dev = mesh.shape["grp"], mesh.shape["dev"]

    def shards(positions, velocities, accel_old, jerk_old, masses, levels, live_count, active_slot):
        n_src, n_act = positions.shape[1], active_slot.shape[0]
        n_chunk = n_src // LANES
        hbm = pl.BlockSpec(memory_space=pltpu.HBM)
        args = (
            positions, velocities, accel_old, jerk_old,
            masses[None], levels[None], live_count, active_slot[None],
        )
        f32 = jnp.float32
        dma = pltpu.SemaphoreType.DMA
        params = {"vmem_limit_bytes": 60 * 1024 * 1024}
        everything = pl.pallas_call(
            functools.partial(share, n_grp, n_dev, math.gcd(2, n_dev), math.gcd(4, n_dev)),
            out_shape=jax.ShapeDtypeStruct((3, 8, n_act), f32),
            in_specs=[hbm] * 8,
            out_specs=hbm,
            scratch_shapes=[
                (pltpu.SMEM if a is live_count else pltpu.VMEM)(a.shape, a.dtype) for a in args
            ] + [
                pltpu.VMEM((n_dev, n_chunk, 8, LANES), f32),
                pltpu.VMEM((n_grp, 8, n_act), f32),
                pltpu.VMEM((n_grp, 6, n_act, LANES), f32),
                pltpu.VMEM((7, n_act, LANES), f32),
                pltpu.VMEM((8, n_src), f32),
                pltpu.VMEM((n_grp, 8, n_act), f32),
                pltpu.VMEM((n_grp, 8, n_act), f32),
                pltpu.VMEM((3, 8, n_act), f32),
                dma((8,)),
                dma((n_dev,)), dma((n_dev,)),
                dma((n_grp,)), dma((n_grp,)),
                dma((n_grp,)), dma((n_grp,)),
                dma,
            ],
            compiler_params=pltpu.CompilerParams(
                collective_id=0, has_side_effects=True, **params
            ),
        )(*args)
        pos_vel, acc_jerk, pot = pl.pallas_call(
            hand_out,
            out_shape=(
                jax.ShapeDtypeStruct((6, n_act), f32),
                jax.ShapeDtypeStruct((6, n_act), f32),
                jax.ShapeDtypeStruct((1, n_act), f32),
            ),
            in_specs=[hbm],
            out_specs=(hbm,) * 3,
            scratch_shapes=[dma((3,))],
            compiler_params=pltpu.CompilerParams(**params),
        )(everything)
        return pos_vel, acc_jerk, pot[0]

    split = P(None, ("grp", "dev"))
    flat = P(("grp", "dev"))
    return jax.shard_map(
        shards,
        mesh=mesh,
        in_specs=(split, split, split, split, flat, flat, flat, flat),
        out_specs=(split, split, flat),
        check_vma=False,
    )
```

```python
import functools
import math

import jax
import jax.numpy as jnp
from jax import lax
from jax.experimental import pallas as pl
from jax.experimental.pallas import tpu as pltpu
from jax.sharding import PartitionSpec as P

MESH = pl.DeviceIdType.MESH
LANES = 128
TAU_BASE = 0.5
SOFTEN_SQ = 0.0001


def add_pairs(state, sums, source):
    x, y, z, vx, vy, vz = state
    ax, ay, az, jx, jy, jz, pot = sums
    sx, sy, sz, svx, svy, svz, mass = source
    dx, dy, dz = sx - x, sy - y, sz - z
    ex, ey, ez = svx - vx, svy - vy, svz - vz
    inv = lax.rsqrt(dx * dx + dy * dy + dz * dz + SOFTEN_SQ)
    inv_sq = inv * inv
    w = mass * inv
    u = w * inv_sq
    radial = (3.0 * inv_sq) * (dx * ex + dy * ey + dz * ez)
    px, py, pz = u * dx, u * dy, u * dz
    return (
        ax + px, ay + py, az + pz,
        jx + (u * ex - radial * px), jy + (u * ey - radial * py), jz + (u * ez - radial * pz),
        pot + w,
    )


def sweep(act, total, rows, fresh, chunks):
    def group(g, carry):
        at = pl.ds(pl.multiple_of(g * rows, rows), rows)
        state = [act[c, at, :] for c in range(6)]
        if fresh:
            sums = (jnp.zeros((rows, LANES), jnp.float32),) * 7
        else:
            sums = tuple(total[c, at, :] for c in range(7))
        for chunk in chunks:
            sums = add_pairs(state, sums, [chunk(c) for c in range(7)])
        for c in range(7):
            total[c, at, :] = sums[c]
        return carry

    lax.fori_loop(0, act.shape[1] // rows, group, 0)


def share(
    n_grp, n_dev, few, many,
    pos_hbm, vel_hbm, acc_hbm, jerk_hbm, mass_hbm, level_hbm, live_hbm, slot_hbm,
    out_hbm,
    pos_ref, vel_ref, acc_ref, jerk_ref, mass_ref, level_ref, live_ref, slot_ref,
    src, stars, act, total, rest, part, gain, out,
    load_sem, src_send, src_recv, star_send, star_recv, part_send, part_recv, out_sem,
):
    n_src = pos_ref.shape[1]
    n_act = slot_ref.shape[1]
    n_chunk = n_src // LANES
    grp, dev = lax.axis_index("grp"), lax.axis_index("dev")

    loads = [
        pltpu.make_async_copy(there, here, load_sem.at[i])
        for i, (there, here) in enumerate((
            (pos_hbm, pos_ref), (vel_hbm, vel_ref), (acc_hbm, acc_ref), (jerk_hbm, jerk_ref),
            (mass_hbm, mass_ref), (level_hbm, level_ref), (live_hbm, live_ref), (slot_hbm, slot_ref),
        ))
    ]
    for load in loads:
        load.start()

    def on_dev(k):
        return lax.rem(dev + k, n_dev)

    def on_grp(k):
        return lax.rem(grp + k, n_grp)

    def each(count, body):
        def one(k, carry):
            body(k)
            return carry

        lax.fori_loop(1, count, one, 0)

    barrier = pltpu.get_barrier_semaphore()

    def greet(place):
        pl.semaphore_signal(barrier, inc=1, device_id=place, device_id_type=MESH)

    each(n_dev, lambda k: greet((grp, on_dev(k))))
    each(n_grp, lambda k: greet((on_grp(k), dev)))
    for load in loads:
        load.wait()

    mine = src.at[dev]
    level = level_ref[...]
    step = jnp.full(level.shape, TAU_BASE, jnp.float32)
    step = jnp.where((level & 1) != 0, step * 0.5, step)
    step = jnp.where((level & 2) != 0, step * 0.25, step)
    step = jnp.where((level & 4) != 0, step * 0.0625, step)
    vel, acc, jerk = vel_ref[...], acc_ref[...], jerk_ref[...]
    pos_pred = pos_ref[...] + step * (vel + step * (acc * 0.5 + step * jerk * (1.0 / 6.0)))
    vel_pred = vel + step * (acc + step * jerk * 0.5)
    lane = lax.broadcasted_iota(jnp.int32, (1, n_src), 1)
    live_mass = jnp.where(lane < live_ref[0], mass_ref[...], 0.0)
    blank = jnp.zeros_like(step)
    for chunk in range(n_chunk):
        cut = slice(chunk * LANES, (chunk + 1) * LANES)
        mine[chunk, 0:3, :] = pos_pred[:, cut]
        mine[chunk, 3:6, :] = vel_pred[:, cut]
        mine[chunk, 6:7, :] = live_mass[:, cut]
        mine[chunk, 7:8, :] = blank[:, cut]
    rest[0:3, :] = acc
    rest[3:6, :] = jerk
    rest[6:7, :] = step
    rest[7:8, :] = blank

    pl.semaphore_wait(barrier, (n_dev - 1) + (n_grp - 1))

    def src_copy(origin, other):
        return pltpu.make_async_remote_copy(
            src_ref=src.at[origin], dst_ref=src.at[origin],
            send_sem=src_send.at[other], recv_sem=src_recv.at[origin],
            device_id=(grp, other), device_id_type=MESH,
        )

    def star_copy(origin, other):
        return pltpu.make_async_remote_copy(
            src_ref=stars.at[origin], dst_ref=stars.at[origin],
            send_sem=star_send.at[other], recv_sem=star_recv.at[origin],
            device_id=(other, dev), device_id_type=MESH,
        )

    def part_copy(origin, other):
        return pltpu.make_async_remote_copy(
            src_ref=part.at[other], dst_ref=gain.at[origin],
            send_sem=part_send.at[other], recv_sem=part_recv.at[origin],
            device_id=(other, dev), device_id_type=MESH,
        )

    each(n_dev, lambda k: src_copy(dev, on_dev(k)).start())

    slot = jnp.broadcast_to(slot_ref[...], (8, n_act))
    low, place = slot & (LANES - 1), slot // LANES

    def pick(chunk_of):
        found = jnp.zeros((8, n_act), jnp.float32)
        for chunk in range(n_chunk):
            here = jnp.take_along_axis(chunk_of(chunk), low, axis=1)
            found = jnp.where(place == chunk, here, found)
        return found

    state = pick(lambda chunk: mine[chunk])
    stars[grp] = state
    each(n_grp, lambda k: star_copy(grp, on_grp(k)).start())
    old = pick(lambda chunk: rest[:, chunk * LANES : (chunk + 1) * LANES])

    def spread(origin):
        columns = stars[origin].T
        for c in range(6):
            act[origin, c] = jnp.broadcast_to(columns[:, c : c + 1], (n_act, LANES))

    spread(grp)

    def meet(k):
        origin = on_grp(k)
        star_copy(origin, origin).wait_recv()
        spread(origin)

    each(n_grp, meet)

    def add(origin, batch, turn, fresh, arriving):
        chunks = []
        for b in range(batch):
            k = turn * batch + b
            index = on_dev(k)
            chunks += [
                lambda c, index=index, chunk=chunk: src[index, chunk, c : c + 1, :]
                for chunk in range(n_chunk)
            ]
            if arriving and not (fresh and b == 0):
                src_copy(index, index).wait_recv()
        sweep(act.at[origin], total, math.gcd(16, n_act), fresh, chunks)

    def add_all(origin, batch, arriving):
        add(origin, batch, 0, True, arriving)

        def turns(turn, carry):
            add(origin, batch, turn, False, arriving)
            return carry

        lax.fori_loop(1, n_dev // batch, turns, 0)

    def summed_up():
        lane = lax.broadcasted_iota(jnp.int32, (n_act, LANES), 1)
        columns = jnp.zeros((n_act, LANES), jnp.float32)
        for c in range(7):
            columns = jnp.where(lane == c, jnp.sum(total[c], axis=1, keepdims=True), columns)
        return columns.T[0:8, :]

    def give(k, batch, arriving):
        origin = on_grp(k)
        add_all(origin, batch, arriving)
        part[origin] = summed_up()
        part_copy(grp, origin).start()

    if n_grp > 1:
        give(1, few, True)

    def give_next(k, carry):
        give(k, many, False)
        return carry

    lax.fori_loop(2, n_grp, give_next, 0)
    add_all(grp, many, n_grp == 1)
    part[grp] = summed_up()

    def gather(k, summed):
        origin = on_grp(k)
        part_copy(origin, origin).wait_recv()
        return summed + gain[origin]

    summed = lax.fori_loop(1, n_grp, gather, part[grp])

    acc_end, jerk_end = summed[0:3], summed[3:6]
    acc_start, jerk_start, h = old[0:3], old[3:6], old[6:7]
    differ = acc_start - acc_end
    fourth = -6.0 * differ - h * (4.0 * jerk_start + 2.0 * jerk_end)
    fifth = 12.0 * differ + 6.0 * h * (jerk_start + jerk_end)
    out[0, 0:3, :] = state[0:3] + h * h * (1.0 / 24.0) * fourth + h * h * (1.0 / 120.0) * fifth
    out[0, 3:6, :] = state[3:6] + h * (1.0 / 6.0) * fourth + h * (1.0 / 24.0) * fifth
    out[0, 6:8, :] = jnp.zeros((2, n_act), jnp.float32)
    out[1] = summed
    out[2] = jnp.broadcast_to(-summed[6:7], (8, n_act))
    out_copy = pltpu.make_async_copy(out, out_hbm, out_sem)
    out_copy.start()
    each(n_dev, lambda k: src_copy(dev, on_dev(k)).wait_send())
    each(n_grp, lambda k: star_copy(grp, on_grp(k)).wait_send())
    each(n_grp, lambda k: part_copy(grp, on_grp(k)).wait_send())
    out_copy.wait()


def hand_out(all_hbm, pos_vel_hbm, acc_jerk_hbm, pot_hbm, sem):
    copies = [
        pltpu.make_async_copy(all_hbm.at[0, 0:6], pos_vel_hbm, sem.at[0]),
        pltpu.make_async_copy(all_hbm.at[1, 0:6], acc_jerk_hbm, sem.at[1]),
        pltpu.make_async_copy(all_hbm.at[2, 0:1], pot_hbm, sem.at[2]),
    ]
    for copy in copies:
        copy.start()
    for copy in copies:
        copy.wait()


def solution(mesh):
    n_grp, n_dev = mesh.shape["grp"], mesh.shape["dev"]

    def shards(positions, velocities, accel_old, jerk_old, masses, levels, live_count, active_slot):
        n_src, n_act = positions.shape[1], active_slot.shape[0]
        n_chunk = n_src // LANES
        hbm = pl.BlockSpec(memory_space=pltpu.HBM)
        args = (
            positions, velocities, accel_old, jerk_old,
            masses[None], levels[None], live_count, active_slot[None],
        )
        f32 = jnp.float32
        dma = pltpu.SemaphoreType.DMA
        params = {"vmem_limit_bytes": 60 * 1024 * 1024}
        everything = pl.pallas_call(
            functools.partial(share, n_grp, n_dev, math.gcd(4, n_dev), math.gcd(8, n_dev)),
            out_shape=jax.ShapeDtypeStruct((3, 8, n_act), f32),
            in_specs=[hbm] * 8,
            out_specs=hbm,
            scratch_shapes=[
                (pltpu.SMEM if a is live_count else pltpu.VMEM)(a.shape, a.dtype) for a in args
            ] + [
                pltpu.VMEM((n_dev, n_chunk, 8, LANES), f32),
                pltpu.VMEM((n_grp, 8, n_act), f32),
                pltpu.VMEM((n_grp, 6, n_act, LANES), f32),
                pltpu.VMEM((7, n_act, LANES), f32),
                pltpu.VMEM((8, n_src), f32),
                pltpu.VMEM((n_grp, 8, n_act), f32),
                pltpu.VMEM((n_grp, 8, n_act), f32),
                pltpu.VMEM((3, 8, n_act), f32),
                dma((8,)),
                dma((n_dev,)), dma((n_dev,)),
                dma((n_grp,)), dma((n_grp,)),
                dma((n_grp,)), dma((n_grp,)),
                dma,
            ],
            compiler_params=pltpu.CompilerParams(
                collective_id=0, has_side_effects=True, **params
            ),
        )(*args)
        pos_vel, acc_jerk, pot = pl.pallas_call(
            hand_out,
            out_shape=(
                jax.ShapeDtypeStruct((6, n_act), f32),
                jax.ShapeDtypeStruct((6, n_act), f32),
                jax.ShapeDtypeStruct((1, n_act), f32),
            ),
            in_specs=[hbm],
            out_specs=(hbm,) * 3,
            scratch_shapes=[dma((3,))],
            compiler_params=pltpu.CompilerParams(**params),
        )(everything)
        return pos_vel, acc_jerk, pot[0]

    split = P(None, ("grp", "dev"))
    flat = P(("grp", "dev"))
    return jax.shard_map(
        shards,
        mesh=mesh,
        in_specs=(split, split, split, split, flat, flat, flat, flat),
        out_specs=(split, split, flat),
        check_vma=False,
    )
```

```python
import functools
import math

import jax
import jax.numpy as jnp
from jax import lax
from jax.experimental import pallas as pl
from jax.experimental.pallas import tpu as pltpu
from jax.sharding import PartitionSpec as P

MESH = pl.DeviceIdType.MESH
LANES = 128
TAU_BASE = 0.5
SOFTEN_SQ = 0.0001


def meet_pairs(state, source):
    x, y, z, vx, vy, vz = state
    sx, sy, sz, svx, svy, svz = source
    dx, dy, dz = sx - x, sy - y, sz - z
    ex, ey, ez = svx - vx, svy - vy, svz - vz
    inv = lax.rsqrt(dx * dx + dy * dy + dz * dz + SOFTEN_SQ)
    return dx, dy, dz, ex, ey, ez, dx * ex + dy * ey + dz * ez, inv


def add_pairs(sums, pairs, mass):
    ax, ay, az, jx, jy, jz, pot = sums
    dx, dy, dz, ex, ey, ez, along, inv = pairs
    inv_sq = inv * inv
    w = mass * inv
    u = w * inv_sq
    radial = (3.0 * inv_sq) * along
    px, py, pz = u * dx, u * dy, u * dz
    return (
        ax + px, ay + py, az + pz,
        jx + (u * ex - radial * px), jy + (u * ey - radial * py), jz + (u * ez - radial * pz),
        pot + w,
    )


def sweep(act, total, rows, n_block, n_chunk, row_of):
    def group(g, carry):
        at = pl.ds(pl.multiple_of(g * rows, rows), rows)
        state = [act[c, at, :] for c in range(6)]

        def met(block, chunk):
            return meet_pairs(state, [row_of(block, chunk, c) for c in range(6)])

        def step(block, held):
            sums, pairs = held
            for chunk in range(n_chunk):
                if chunk + 1 < n_chunk:
                    later = met(block, chunk + 1)
                else:
                    later = met(block + 1, 0)
                sums = add_pairs(sums, pairs, row_of(block, chunk, 6))
                pairs = later
            return sums, pairs

        nothing = (jnp.zeros((rows, LANES), jnp.float32),) * 7
        sums, _ = lax.fori_loop(0, n_block, step, (nothing, met(0, 0)))
        for c in range(7):
            total[c, at, :] = sums[c]
        return carry

    lax.fori_loop(0, act.shape[1] // rows, group, 0)


def share(
    n_grp, n_dev,
    pos_hbm, vel_hbm, acc_hbm, jerk_hbm, mass_hbm, level_hbm, live_hbm, slot_hbm,
    out_hbm,
    pos_ref, vel_ref, acc_ref, jerk_ref, mass_ref, level_ref, live_ref, slot_ref,
    src, stars, act, total, rest, part, gain, out,
    load_sem, src_send, src_recv, star_send, star_recv, part_send, part_recv, out_sem,
):
    n_src = pos_ref.shape[1]
    n_act = slot_ref.shape[1]
    n_chunk = n_src // LANES
    grp, dev = lax.axis_index("grp"), lax.axis_index("dev")

    loads = [
        pltpu.make_async_copy(there, here, load_sem.at[i])
        for i, (there, here) in enumerate((
            (pos_hbm, pos_ref), (vel_hbm, vel_ref), (acc_hbm, acc_ref), (jerk_hbm, jerk_ref),
            (mass_hbm, mass_ref), (level_hbm, level_ref), (live_hbm, live_ref), (slot_hbm, slot_ref),
        ))
    ]
    for load in loads:
        load.start()

    def on_dev(k):
        return lax.rem(dev + k, n_dev)

    def on_grp(k):
        return lax.rem(grp + k, n_grp)

    def each(count, body):
        def one(k, carry):
            body(k)
            return carry

        lax.fori_loop(1, count, one, 0)

    barrier = pltpu.get_barrier_semaphore()

    def greet(place):
        pl.semaphore_signal(barrier, inc=1, device_id=place, device_id_type=MESH)

    each(n_dev, lambda k: greet((grp, on_dev(k))))
    each(n_grp, lambda k: greet((on_grp(k), dev)))
    for load in loads:
        load.wait()

    mine = src.at[dev]
    level = level_ref[...]
    step = jnp.full(level.shape, TAU_BASE, jnp.float32)
    step = jnp.where((level & 1) != 0, step * 0.5, step)
    step = jnp.where((level & 2) != 0, step * 0.25, step)
    step = jnp.where((level & 4) != 0, step * 0.0625, step)
    vel, acc, jerk = vel_ref[...], acc_ref[...], jerk_ref[...]
    pos_pred = pos_ref[...] + step * (vel + step * (acc * 0.5 + step * jerk * (1.0 / 6.0)))
    vel_pred = vel + step * (acc + step * jerk * 0.5)
    lane = lax.broadcasted_iota(jnp.int32, (1, n_src), 1)
    live_mass = jnp.where(lane < live_ref[0], mass_ref[...], 0.0)
    blank = jnp.zeros_like(step)
    for chunk in range(n_chunk):
        cut = slice(chunk * LANES, (chunk + 1) * LANES)
        mine[chunk, 0:3, :] = pos_pred[:, cut]
        mine[chunk, 3:6, :] = vel_pred[:, cut]
        mine[chunk, 6:7, :] = live_mass[:, cut]
        mine[chunk, 7:8, :] = blank[:, cut]
    rest[0:3, :] = acc
    rest[3:6, :] = jerk
    rest[6:7, :] = step
    rest[7:8, :] = blank

    pl.semaphore_wait(barrier, (n_dev - 1) + (n_grp - 1))

    def src_copy(origin, other):
        return pltpu.make_async_remote_copy(
            src_ref=src.at[origin], dst_ref=src.at[origin],
            send_sem=src_send.at[other], recv_sem=src_recv.at[origin],
            device_id=(grp, other), device_id_type=MESH,
        )

    def star_copy(origin, other):
        return pltpu.make_async_remote_copy(
            src_ref=stars.at[origin], dst_ref=stars.at[origin],
            send_sem=star_send.at[other], recv_sem=star_recv.at[origin],
            device_id=(other, dev), device_id_type=MESH,
        )

    def part_copy(origin, other):
        return pltpu.make_async_remote_copy(
            src_ref=part.at[other], dst_ref=gain.at[origin],
            send_sem=part_send.at[other], recv_sem=part_recv.at[origin],
            device_id=(other, dev), device_id_type=MESH,
        )

    each(n_dev, lambda k: src_copy(dev, on_dev(k)).start())

    slot = jnp.broadcast_to(slot_ref[...], (8, n_act))
    low, place = slot & (LANES - 1), slot // LANES

    def pick(chunk_of):
        found = jnp.zeros((8, n_act), jnp.float32)
        for chunk in range(n_chunk):
            here = jnp.take_along_axis(chunk_of(chunk), low, axis=1)
            found = jnp.where(place == chunk, here, found)
        return found

    state = pick(lambda chunk: mine[chunk])
    stars[grp] = state
    each(n_grp, lambda k: star_copy(grp, on_grp(k)).start())
    old = pick(lambda chunk: rest[:, chunk * LANES : (chunk + 1) * LANES])

    def spread(origin):
        columns = stars[origin].T
        for c in range(6):
            act[origin, c] = jnp.broadcast_to(columns[:, c : c + 1], (n_act, LANES))

    spread(grp)

    def meet(k):
        origin = on_grp(k)
        star_copy(origin, origin).wait_recv()
        spread(origin)

    each(n_grp, meet)

    def add_all(origin):
        sweep(
            act.at[origin], total, math.gcd(16, n_act), n_dev, n_chunk,
            lambda block, chunk, c: src[on_dev(block), chunk, c : c + 1, :],
        )

    def summed_up():
        lane = lax.broadcasted_iota(jnp.int32, (n_act, LANES), 1)
        columns = jnp.zeros((n_act, LANES), jnp.float32)
        for c in range(7):
            columns = jnp.where(lane == c, jnp.sum(total[c], axis=1, keepdims=True), columns)
        return columns.T[0:8, :]

    each(n_dev, lambda k: src_copy(on_dev(k), on_dev(k)).wait_recv())

    def give(k):
        origin = on_grp(k)
        add_all(origin)
        part[origin] = summed_up()
        part_copy(grp, origin).start()

    each(n_grp, give)
    add_all(grp)
    part[grp] = summed_up()

    def gather(k, summed):
        origin = on_grp(k)
        part_copy(origin, origin).wait_recv()
        return summed + gain[origin]

    summed = lax.fori_loop(1, n_grp, gather, part[grp])

    acc_end, jerk_end = summed[0:3], summed[3:6]
    acc_start, jerk_start, h = old[0:3], old[3:6], old[6:7]
    differ = acc_start - acc_end
    fourth = -6.0 * differ - h * (4.0 * jerk_start + 2.0 * jerk_end)
    fifth = 12.0 * differ + 6.0 * h * (jerk_start + jerk_end)
    out[0, 0:3, :] = state[0:3] + h * h * (1.0 / 24.0) * fourth + h * h * (1.0 / 120.0) * fifth
    out[0, 3:6, :] = state[3:6] + h * (1.0 / 6.0) * fourth + h * (1.0 / 24.0) * fifth
    out[0, 6:8, :] = jnp.zeros((2, n_act), jnp.float32)
    out[1] = summed
    out[2] = jnp.broadcast_to(-summed[6:7], (8, n_act))
    out_copy = pltpu.make_async_copy(out, out_hbm, out_sem)
    out_copy.start()
    each(n_dev, lambda k: src_copy(dev, on_dev(k)).wait_send())
    each(n_grp, lambda k: star_copy(grp, on_grp(k)).wait_send())
    each(n_grp, lambda k: part_copy(grp, on_grp(k)).wait_send())
    out_copy.wait()


def hand_out(all_hbm, pos_vel_hbm, acc_jerk_hbm, pot_hbm, sem):
    copies = [
        pltpu.make_async_copy(all_hbm.at[0, 0:6], pos_vel_hbm, sem.at[0]),
        pltpu.make_async_copy(all_hbm.at[1, 0:6], acc_jerk_hbm, sem.at[1]),
        pltpu.make_async_copy(all_hbm.at[2, 0:1], pot_hbm, sem.at[2]),
    ]
    for copy in copies:
        copy.start()
    for copy in copies:
        copy.wait()


def solution(mesh):
    n_grp, n_dev = mesh.shape["grp"], mesh.shape["dev"]

    def shards(positions, velocities, accel_old, jerk_old, masses, levels, live_count, active_slot):
        n_src, n_act = positions.shape[1], active_slot.shape[0]
        n_chunk = n_src // LANES
        hbm = pl.BlockSpec(memory_space=pltpu.HBM)
        args = (
            positions, velocities, accel_old, jerk_old,
            masses[None], levels[None], live_count, active_slot[None],
        )
        f32 = jnp.float32
        dma = pltpu.SemaphoreType.DMA
        params = {"vmem_limit_bytes": 60 * 1024 * 1024}
        everything = pl.pallas_call(
            functools.partial(share, n_grp, n_dev),
            out_shape=jax.ShapeDtypeStruct((3, 8, n_act), f32),
            in_specs=[hbm] * 8,
            out_specs=hbm,
            scratch_shapes=[
                (pltpu.SMEM if a is live_count else pltpu.VMEM)(a.shape, a.dtype) for a in args
            ] + [
                pltpu.VMEM((n_dev, n_chunk, 8, LANES), f32),
                pltpu.VMEM((n_grp, 8, n_act), f32),
                pltpu.VMEM((n_grp, 6, n_act, LANES), f32),
                pltpu.VMEM((7, n_act, LANES), f32),
                pltpu.VMEM((8, n_src), f32),
                pltpu.VMEM((n_grp, 8, n_act), f32),
                pltpu.VMEM((n_grp, 8, n_act), f32),
                pltpu.VMEM((3, 8, n_act), f32),
                dma((8,)),
                dma((n_dev,)), dma((n_dev,)),
                dma((n_grp,)), dma((n_grp,)),
                dma((n_grp,)), dma((n_grp,)),
                dma,
            ],
            compiler_params=pltpu.CompilerParams(
                collective_id=0, has_side_effects=True, **params
            ),
        )(*args)
        pos_vel, acc_jerk, pot = pl.pallas_call(
            hand_out,
            out_shape=(
                jax.ShapeDtypeStruct((6, n_act), f32),
                jax.ShapeDtypeStruct((6, n_act), f32),
                jax.ShapeDtypeStruct((1, n_act), f32),
            ),
            in_specs=[hbm],
            out_specs=(hbm,) * 3,
            scratch_shapes=[dma((3,))],
            compiler_params=pltpu.CompilerParams(**params),
        )(everything)
        return pos_vel, acc_jerk, pot[0]

    split = P(None, ("grp", "dev"))
    flat = P(("grp", "dev"))
    return jax.shard_map(
        shards,
        mesh=mesh,
        in_specs=(split, split, split, split, flat, flat, flat, flat),
        out_specs=(split, split, flat),
        check_vma=False,
    )
```

```python
import functools
import math

import jax
import jax.numpy as jnp
from jax import lax
from jax.experimental import pallas as pl
from jax.experimental.pallas import tpu as pltpu
from jax.sharding import PartitionSpec as P

MESH = pl.DeviceIdType.MESH
LANES = 128
TAU_BASE = 0.5
SOFTEN_SQ = 0.0001


def add_pairs(state, sums, source):
    x, y, z, vx, vy, vz = state
    ax, ay, az, jx, jy, jz, pot = sums
    sx, sy, sz, svx, svy, svz, mass = source
    dx, dy, dz = sx - x, sy - y, sz - z
    ex, ey, ez = svx - vx, svy - vy, svz - vz
    inv = lax.rsqrt(dx * dx + dy * dy + dz * dz + SOFTEN_SQ)
    inv_sq = inv * inv
    w = mass * inv
    u = w * inv_sq
    radial = (3.0 * inv_sq) * (dx * ex + dy * ey + dz * ez)
    px, py, pz = u * dx, u * dy, u * dz
    return (
        ax + px, ay + py, az + pz,
        jx + (u * ex - radial * px), jy + (u * ey - radial * py), jz + (u * ez - radial * pz),
        pot + w,
    )


def sweep(act, total, rows, chunks):
    def group(g, carry):
        at = pl.ds(pl.multiple_of(g * rows, rows), rows)
        state = [act[c, at, :] for c in range(6)]
        sums = tuple(total[c, at, :] for c in range(7))
        for chunk in chunks:
            sums = add_pairs(state, sums, [chunk(c) for c in range(7)])
        for c in range(7):
            total[c, at, :] = sums[c]
        return carry

    lax.fori_loop(0, act.shape[1] // rows, group, 0)


def spread(own, act):
    for c in range(6):
        act[c] = jnp.broadcast_to(own[c : c + 1, :], (LANES, own.shape[1])).T


def share(
    n_grp, n_line, n_core, rows, batch,
    pos_hbm, vel_hbm, acc_hbm, jerk_hbm, mass_hbm, level_hbm, live_hbm, slot_hbm,
    beyond_hbm, total_hbm, own_hbm,
    pos_ref, vel_ref, acc_ref, jerk_ref, mass_ref, level_ref, live_ref, slot_ref,
    src, act, total, own, rest,
    load_sem, line_send, line_recv, grp_send, grp_recv, core_send, core_recv, beyond_sem, out_sem,
):
    n_src = pos_ref.shape[1]
    n_act = slot_ref.shape[1]
    n_chunk = n_src // LANES
    grp = lax.axis_index("grp")
    dev = lax.axis_index("dev")
    line, core = dev // n_core, lax.rem(dev, n_core)
    twin = n_core - 1 - core

    loads = [
        pltpu.make_async_copy(there, here, load_sem.at[i])
        for i, (there, here) in enumerate((
            (pos_hbm, pos_ref), (vel_hbm, vel_ref), (acc_hbm, acc_ref), (jerk_hbm, jerk_ref),
            (mass_hbm, mass_ref), (level_hbm, level_ref), (live_hbm, live_ref), (slot_hbm, slot_ref),
        ))
    ]
    for load in loads:
        load.start()

    def on_line(k):
        return lax.rem(line + k, n_line)

    def on_grp(k):
        return lax.rem(grp + k, n_grp)

    def each(count, body):
        def one(k, carry):
            body(k)
            return carry

        lax.fori_loop(1, count, one, 0)

    barrier = pltpu.get_barrier_semaphore()

    def greet(place):
        pl.semaphore_signal(barrier, inc=1, device_id=place, device_id_type=MESH)

    each(n_line, lambda k: greet((grp, on_line(k) * n_core + core)))
    each(n_grp, lambda k: greet((on_grp(k), dev)))
    if n_core > 1:
        greet((grp, line * n_core + twin))
    total[...] = jnp.zeros_like(total)
    for load in loads:
        load.wait()

    mine = src.at[core, grp, line]
    level = level_ref[...]
    step = jnp.full(level.shape, TAU_BASE, jnp.float32)
    step = jnp.where((level & 1) != 0, step * 0.5, step)
    step = jnp.where((level & 2) != 0, step * 0.25, step)
    step = jnp.where((level & 4) != 0, step * 0.0625, step)
    vel, acc, jerk = vel_ref[...], acc_ref[...], jerk_ref[...]
    pos_pred = pos_ref[...] + step * (vel + step * (acc * 0.5 + step * jerk * (1.0 / 6.0)))
    vel_pred = vel + step * (acc + step * jerk * 0.5)
    lane = lax.broadcasted_iota(jnp.int32, (1, n_src), 1)
    live = jnp.full((1, n_src), live_ref[0], jnp.int32)
    live_mass = jnp.where(lane < live, mass_ref[...], 0.0)
    count = live.astype(jnp.float32)
    for chunk in range(n_chunk):
        cut = slice(chunk * LANES, (chunk + 1) * LANES)
        mine[chunk, 0:3, :] = pos_pred[:, cut]
        mine[chunk, 3:6, :] = vel_pred[:, cut]
        mine[chunk, 6:7, :] = live_mass[:, cut]
        mine[chunk, 7:8, :] = count[:, cut]
    rest[0:3, :] = acc
    rest[3:6, :] = jerk
    rest[6:7, :] = step
    rest[7:8, :] = jnp.zeros_like(step)

    pl.semaphore_wait(barrier, (n_line - 1) + (n_grp - 1) + (n_core - 1))

    def line_copy(origin, other):
        block = src.at[core, grp, origin]
        return pltpu.make_async_remote_copy(
            src_ref=block, dst_ref=block,
            send_sem=line_send.at[other], recv_sem=line_recv.at[origin],
            device_id=(grp, other * n_core + core), device_id_type=MESH,
        )

    def grp_copy(at, origin, other):
        block = src.at[core, origin, at]
        return pltpu.make_async_remote_copy(
            src_ref=block, dst_ref=block,
            send_sem=grp_send.at[at, other], recv_sem=grp_recv.at[at, origin],
            device_id=(other, dev), device_id_type=MESH,
        )

    def to_groups(at):
        each(n_grp, lambda k: grp_copy(at, grp, on_grp(k)).start())

    def core_copy(owner, origin):
        block = src.at[owner, origin]
        return pltpu.make_async_remote_copy(
            src_ref=block, dst_ref=block,
            send_sem=core_send.at[origin], recv_sem=core_recv.at[origin],
            device_id=(grp, line * n_core + twin), device_id_type=MESH,
        )

    def keep(owner, origin):
        return pltpu.make_async_copy(
            src.at[owner, origin, :, 1:], beyond_hbm.at[owner, origin], beyond_sem.at[owner, origin]
        )

    def add(owner, origin):
        def turn(t, carry):
            sweep(act, total, rows, [
                lambda c, at=t * batch + b: src[owner, origin, at, 0, c : c + 1, :]
                for b in range(batch)
            ])
            return carry

        lax.fori_loop(0, n_line // batch, turn, 0)

    each(n_line, lambda k: line_copy(line, on_line(k)).start())
    to_groups(line)

    slot = jnp.broadcast_to(slot_ref[...], (8, n_act))
    low, part = slot & (LANES - 1), slot // LANES

    def pick(chunk_of):
        out = jnp.zeros((8, n_act), jnp.float32)
        for chunk in range(n_chunk):
            found = jnp.take_along_axis(chunk_of(chunk), low, axis=1)
            out = jnp.where(part == chunk, found, out)
        return out

    state = pick(lambda chunk: mine[chunk])
    own[0:8, :] = state
    own[8:16, :] = pick(lambda chunk: rest[:, chunk * LANES : (chunk + 1) * LANES])
    own_copy = pltpu.make_async_copy(own, own_hbm, out_sem.at[0])
    own_copy.start()
    spread(own, act)

    def pass_on(k):
        line_copy(on_line(k), on_line(k)).wait_recv()
        to_groups(on_line(k))

    each(n_line, pass_on)
    if n_core > 1:
        core_copy(core, grp).start()
    keep(core, grp).start()
    add(core, grp)
    if n_core > 1:
        core_copy(twin, grp).wait_recv()
        keep(twin, grp).start()
        add(twin, grp)

    def forward(k):
        origin = on_grp(k)
        grp_copy(line, origin, origin).wait_recv()
        each(n_line, lambda at: grp_copy(on_line(at), origin, origin).wait_recv())
        if n_core > 1:
            core_copy(core, origin).start()
        keep(core, origin).start()

    each(n_grp, forward)
    each(n_grp, lambda k: add(core, on_grp(k)))

    if n_core > 1:
        def last(k):
            origin = on_grp(k)
            core_copy(twin, origin).wait_recv()
            keep(twin, origin).start()
            add(twin, origin)

        each(n_grp, last)

    total_copy = pltpu.make_async_copy(total, total_hbm, out_sem.at[1])
    total_copy.start()
    each(n_line, lambda k: line_copy(line, on_line(k)).wait_send())

    def sent(at, carry):
        each(n_grp, lambda k: grp_copy(at, grp, on_grp(k)).wait_send())
        return carry

    lax.fori_loop(0, n_line, sent, 0)

    def settle(origin, carry):
        if n_core > 1:
            core_copy(core, origin).wait_send()
        for owner in range(n_core):
            keep(owner, origin).wait()
        return carry

    lax.fori_loop(0, n_grp, settle, 0)
    own_copy.wait()
    total_copy.wait()


def finish(
    rows, batch,
    beyond_hbm, total_hbm, own_hbm,
    pos_vel_hbm, acc_jerk_hbm, pot_hbm,
    beyond, total, own, act, packed, more, pos_vel_ref, acc_jerk_ref, pot_ref, load_sem, store_sem,
):
    n, n_beyond = beyond.shape[0], beyond.shape[1]
    loads = [
        pltpu.make_async_copy(there, here, load_sem.at[i])
        for i, (there, here) in enumerate(((own_hbm, own), (beyond_hbm, beyond), (total_hbm, total)))
    ]
    for load in loads:
        load.start()
    lane = lax.broadcasted_iota(jnp.int32, (8, LANES), 1)
    row = lax.broadcasted_iota(jnp.int32, (8, LANES), 0)
    more[...] = jnp.zeros_like(more)
    loads[0].wait()
    spread(own, act)
    loads[1].wait()

    unroll = math.gcd(8, n)

    def pack(turn, carry):
        filled, now = carry
        counts = [beyond[turn * unroll + b, 0, 7, 0].astype(jnp.int32) for b in range(unroll)]
        for b in range(unroll):
            for chunk in range(n_beyond):
                many = jnp.minimum(jnp.maximum(counts[b] - (chunk + 1) * LANES, 0), LANES)
                start = lax.rem(filled, LANES)
                moved = pltpu.roll(beyond[turn * unroll + b, chunk], start, 1)
                now = jnp.where(lane >= start, moved, now)
                packed[filled // LANES] = now
                now = jnp.where(start + many >= LANES, moved, now)
                filled = filled + many
        return filled, now

    filled, now = lax.fori_loop(
        0, n // unroll, pack, (jnp.int32(0), jnp.zeros((8, LANES), jnp.float32))
    )
    last = filled // LANES
    packed[last] = jnp.where((row == 6) & (lane >= lax.rem(filled, LANES)), 0.0, now)
    for b in range(1, batch):
        packed[last + b] = jnp.zeros((8, LANES), jnp.float32)

    def turns(turn, carry):
        sweep(act, more, rows, [
            lambda c, at=turn * batch + b: packed[at, c : c + 1, :] for b in range(batch)
        ])
        return carry

    lax.fori_loop(0, (filled + batch * LANES - 1) // (batch * LANES), turns, 0)

    loads[2].wait()
    for c in range(6):
        acc_jerk_ref[c : c + 1, :] = jnp.sum((total[c] + more[c]).T, axis=0, keepdims=True)
    pot_ref[...] = -jnp.sum((total[6] + more[6]).T, axis=0, keepdims=True)
    stores = [
        pltpu.make_async_copy(here, there, store_sem.at[i])
        for i, (here, there) in enumerate((
            (acc_jerk_ref, acc_jerk_hbm), (pot_ref, pot_hbm), (pos_vel_ref, pos_vel_hbm),
        ))
    ]
    stores[0].start()
    stores[1].start()

    acc_end, jerk_end = acc_jerk_ref[0:3, :], acc_jerk_ref[3:6, :]
    pos_now, vel_now = own[0:3, :], own[3:6, :]
    acc_start, jerk_start, h = own[8:11, :], own[11:14, :], own[14:15, :]
    differ = acc_start - acc_end
    fourth = -6.0 * differ - h * (4.0 * jerk_start + 2.0 * jerk_end)
    fifth = 12.0 * differ + 6.0 * h * (jerk_start + jerk_end)
    pos_vel_ref[0:3, :] = pos_now + h * h * (1.0 / 24.0) * fourth + h * h * (1.0 / 120.0) * fifth
    pos_vel_ref[3:6, :] = vel_now + h * (1.0 / 6.0) * fourth + h * (1.0 / 24.0) * fifth
    stores[2].start()
    for store in stores:
        store.wait()


def solution(mesh):
    n_grp, n_dev = mesh.shape["grp"], mesh.shape["dev"]
    n = n_grp * n_dev

    def shards(positions, velocities, accel_old, jerk_old, masses, levels, live_count, active_slot):
        n_src, n_act = positions.shape[1], active_slot.shape[0]
        n_chunk = n_src // LANES
        hbm = pl.BlockSpec(memory_space=pltpu.HBM)
        args = (
            positions, velocities, accel_old, jerk_old,
            masses[None], levels[None], live_count, active_slot[None],
        )
        f32 = jnp.float32
        n_core = math.gcd(2, n_dev)
        n_line = n_dev // n_core
        dma = pltpu.SemaphoreType.DMA
        beyond, total, own = pl.pallas_call(
            functools.partial(
                share, n_grp, n_line, n_core, math.gcd(16, n_act), math.gcd(4, n_line)
            ),
            out_shape=(
                jax.ShapeDtypeStruct((n_core, n_grp, n_line, n_chunk - 1, 8, LANES), f32),
                jax.ShapeDtypeStruct((7, n_act, LANES), f32),
                jax.ShapeDtypeStruct((16, n_act), f32),
            ),
            in_specs=[hbm] * 8,
            out_specs=(hbm,) * 3,
            scratch_shapes=[
                (pltpu.SMEM if a is live_count else pltpu.VMEM)(a.shape, a.dtype) for a in args
            ] + [
                pltpu.VMEM((n_core, n_grp, n_line, n_chunk, 8, LANES), f32),
                pltpu.VMEM((6, n_act, LANES), f32),
                pltpu.VMEM((7, n_act, LANES), f32),
                pltpu.VMEM((16, n_act), f32),
                pltpu.VMEM((8, n_src), f32),
                dma((8,)),
                dma((n_line,)), dma((n_line,)),
                dma((n_line, n_grp)), dma((n_line, n_grp)),
                dma((n_grp,)), dma((n_grp,)),
                dma((n_core, n_grp)),
                dma((2,)),
            ],
            compiler_params=pltpu.CompilerParams(
                collective_id=0, has_side_effects=True, vmem_limit_bytes=60 * 1024 * 1024
            ),
        )(*args)
        batch = 2
        pos_vel, acc_jerk, pot = pl.pallas_call(
            functools.partial(finish, math.gcd(32, n_act), batch),
            out_shape=(
                jax.ShapeDtypeStruct((6, n_act), f32),
                jax.ShapeDtypeStruct((6, n_act), f32),
                jax.ShapeDtypeStruct((1, n_act), f32),
            ),
            in_specs=[hbm] * 3,
            out_specs=(hbm,) * 3,
            scratch_shapes=[
                pltpu.VMEM((n, n_chunk - 1, 8, LANES), f32),
                pltpu.VMEM((7, n_act, LANES), f32),
                pltpu.VMEM((16, n_act), f32),
                pltpu.VMEM((6, n_act, LANES), f32),
                pltpu.VMEM((n * (n_chunk - 1) + batch, 8, LANES), f32),
                pltpu.VMEM((7, n_act, LANES), f32),
                pltpu.VMEM((6, n_act), f32),
                pltpu.VMEM((6, n_act), f32),
                pltpu.VMEM((1, n_act), f32),
                dma((3,)),
                dma((3,)),
            ],
            compiler_params=pltpu.CompilerParams(vmem_limit_bytes=60 * 1024 * 1024),
        )(beyond.reshape(n, n_chunk - 1, 8, LANES), total, own)
        return pos_vel, acc_jerk, pot[0]

    split = P(None, ("grp", "dev"))
    flat = P(("grp", "dev"))
    return jax.shard_map(
        shards,
        mesh=mesh,
        in_specs=(split, split, split, split, flat, flat, flat, flat),
        out_specs=(split, split, flat),
        check_vma=False,
    )
```

```python
import functools
import math

import jax
import jax.numpy as jnp
from jax import lax
from jax.experimental import pallas as pl
from jax.experimental.pallas import tpu as pltpu
from jax.sharding import PartitionSpec as P

MESH = pl.DeviceIdType.MESH
LANES = 128
TAU_BASE = 0.5
SOFTEN_SQ = 0.0001


def add_pairs(state, sums, source):
    x, y, z, vx, vy, vz = state
    ax, ay, az, jx, jy, jz, pot = sums
    sx, sy, sz, svx, svy, svz, mass = source
    dx, dy, dz = sx - x, sy - y, sz - z
    ex, ey, ez = svx - vx, svy - vy, svz - vz
    inv = lax.rsqrt(dx * dx + dy * dy + dz * dz + SOFTEN_SQ)
    inv_sq = inv * inv
    w = mass * inv
    u = w * inv_sq
    radial = (3.0 * inv_sq) * (dx * ex + dy * ey + dz * ez)
    px, py, pz = u * dx, u * dy, u * dz
    return (
        ax + px, ay + py, az + pz,
        jx + (u * ex - radial * px), jy + (u * ey - radial * py), jz + (u * ez - radial * pz),
        pot + w,
    )


def sweep(act, total, rows, chunks):
    def group(g, carry):
        at = pl.ds(pl.multiple_of(g * rows, rows), rows)
        state = [act[c, at, :] for c in range(6)]
        sums = tuple(total[c, at, :] for c in range(7))
        for chunk in chunks:
            sums = add_pairs(state, sums, [chunk(c) for c in range(7)])
        for c in range(7):
            total[c, at, :] = sums[c]
        return carry

    lax.fori_loop(0, act.shape[1] // rows, group, 0)


def spread(own, act):
    for c in range(6):
        act[c] = jnp.broadcast_to(own[c : c + 1, :], (LANES, own.shape[1])).T


def share(
    n_grp, n_line, n_core, rows, batch,
    pos_hbm, vel_hbm, acc_hbm, jerk_hbm, mass_hbm, level_hbm, live_hbm, slot_hbm,
    beyond_hbm, total_hbm, own_hbm,
    pos_ref, vel_ref, acc_ref, jerk_ref, mass_ref, level_ref, live_ref, slot_ref,
    src, act, total, own, rest,
    load_sem, line_send, line_recv, grp_send, grp_recv, core_send, core_recv, beyond_sem, out_sem,
):
    n_src = pos_ref.shape[1]
    n_act = slot_ref.shape[1]
    n_chunk = n_src // LANES
    grp = lax.axis_index("grp")
    dev = lax.axis_index("dev")
    line, core = dev // n_core, lax.rem(dev, n_core)
    twin = n_core - 1 - core

    loads = [
        pltpu.make_async_copy(there, here, load_sem.at[i])
        for i, (there, here) in enumerate((
            (pos_hbm, pos_ref), (vel_hbm, vel_ref), (acc_hbm, acc_ref), (jerk_hbm, jerk_ref),
            (mass_hbm, mass_ref), (level_hbm, level_ref), (live_hbm, live_ref), (slot_hbm, slot_ref),
        ))
    ]
    for load in loads:
        load.start()

    def on_line(k):
        return lax.rem(line + k, n_line)

    def on_grp(k):
        return lax.rem(grp + k, n_grp)

    def each(count, body):
        def one(k, carry):
            body(k)
            return carry

        lax.fori_loop(1, count, one, 0)

    barrier = pltpu.get_barrier_semaphore()

    def greet(place):
        pl.semaphore_signal(barrier, inc=1, device_id=place, device_id_type=MESH)

    each(n_line, lambda k: greet((grp, on_line(k) * n_core + core)))
    each(n_grp, lambda k: greet((on_grp(k), dev)))
    if n_core > 1:
        greet((grp, line * n_core + twin))
    total[...] = jnp.zeros_like(total)
    for load in loads:
        load.wait()

    mine = src.at[core, grp, line]
    level = level_ref[...]
    step = jnp.full(level.shape, TAU_BASE, jnp.float32)
    step = jnp.where((level & 1) != 0, step * 0.5, step)
    step = jnp.where((level & 2) != 0, step * 0.25, step)
    step = jnp.where((level & 4) != 0, step * 0.0625, step)
    vel, acc, jerk = vel_ref[...], acc_ref[...], jerk_ref[...]
    pos_pred = pos_ref[...] + step * (vel + step * (acc * 0.5 + step * jerk * (1.0 / 6.0)))
    vel_pred = vel + step * (acc + step * jerk * 0.5)
    lane = lax.broadcasted_iota(jnp.int32, (1, n_src), 1)
    live = jnp.full((1, n_src), live_ref[0], jnp.int32)
    live_mass = jnp.where(lane < live, mass_ref[...], 0.0)
    count = live.astype(jnp.float32)
    for chunk in range(n_chunk):
        cut = slice(chunk * LANES, (chunk + 1) * LANES)
        mine[chunk, 0:3, :] = pos_pred[:, cut]
        mine[chunk, 3:6, :] = vel_pred[:, cut]
        mine[chunk, 6:7, :] = live_mass[:, cut]
        mine[chunk, 7:8, :] = count[:, cut]
    rest[0:3, :] = acc
    rest[3:6, :] = jerk
    rest[6:7, :] = step
    rest[7:8, :] = jnp.zeros_like(step)

    pl.semaphore_wait(barrier, (n_line - 1) + (n_grp - 1) + (n_core - 1))

    def line_copy(origin, other):
        block = src.at[core, grp, origin]
        return pltpu.make_async_remote_copy(
            src_ref=block, dst_ref=block,
            send_sem=line_send.at[other], recv_sem=line_recv.at[origin],
            device_id=(grp, other * n_core + core), device_id_type=MESH,
        )

    def grp_copy(at, origin, other):
        block = src.at[core, origin, at]
        return pltpu.make_async_remote_copy(
            src_ref=block, dst_ref=block,
            send_sem=grp_send.at[at, other], recv_sem=grp_recv.at[at, origin],
            device_id=(other, dev), device_id_type=MESH,
        )

    def to_groups(at):
        each(n_grp, lambda k: grp_copy(at, grp, on_grp(k)).start())

    def core_copy(owner, origin):
        block = src.at[owner, origin]
        return pltpu.make_async_remote_copy(
            src_ref=block, dst_ref=block,
            send_sem=core_send.at[origin], recv_sem=core_recv.at[origin],
            device_id=(grp, line * n_core + twin), device_id_type=MESH,
        )

    def keep(owner, origin):
        return pltpu.make_async_copy(
            src.at[owner, origin, :, 1:], beyond_hbm.at[owner, origin], beyond_sem.at[owner, origin]
        )

    def add(owner, origin):
        def turn(t, carry):
            sweep(act, total, rows, [
                lambda c, at=t * batch + b: src[owner, origin, at, 0, c : c + 1, :]
                for b in range(batch)
            ])
            return carry

        lax.fori_loop(0, n_line // batch, turn, 0)

    def add_others(owner):
        def turn(t, carry):
            sweep(act, total, math.gcd(8, n_act), [
                lambda c, origin=on_grp(k), at=t * batch + b: src[owner, origin, at, 0, c : c + 1, :]
                for k in range(1, n_grp)
                for b in range(batch)
            ])
            return carry

        if n_grp > 1:
            lax.fori_loop(0, n_line // batch, turn, 0)

    each(n_line, lambda k: line_copy(line, on_line(k)).start())
    to_groups(line)

    slot = jnp.broadcast_to(slot_ref[...], (8, n_act))
    low, part = slot & (LANES - 1), slot // LANES

    def pick(chunk_of):
        out = jnp.zeros((8, n_act), jnp.float32)
        for chunk in range(n_chunk):
            found = jnp.take_along_axis(chunk_of(chunk), low, axis=1)
            out = jnp.where(part == chunk, found, out)
        return out

    state = pick(lambda chunk: mine[chunk])
    own[0:8, :] = state
    own[8:16, :] = pick(lambda chunk: rest[:, chunk * LANES : (chunk + 1) * LANES])
    own_copy = pltpu.make_async_copy(own, own_hbm, out_sem.at[0])
    own_copy.start()
    spread(own, act)

    def pass_on(k):
        line_copy(on_line(k), on_line(k)).wait_recv()
        to_groups(on_line(k))

    each(n_line, pass_on)
    if n_core > 1:
        core_copy(core, grp).start()
    keep(core, grp).start()
    add(core, grp)
    if n_core > 1:
        core_copy(twin, grp).wait_recv()
        keep(twin, grp).start()
        add(twin, grp)

    def forward(k):
        origin = on_grp(k)
        grp_copy(line, origin, origin).wait_recv()
        each(n_line, lambda at: grp_copy(on_line(at), origin, origin).wait_recv())
        if n_core > 1:
            core_copy(core, origin).start()
        keep(core, origin).start()

    each(n_grp, forward)
    add_others(core)

    if n_core > 1:
        def last(k):
            origin = on_grp(k)
            core_copy(twin, origin).wait_recv()
            keep(twin, origin).start()

        each(n_grp, last)
        add_others(twin)

    total_copy = pltpu.make_async_copy(total, total_hbm, out_sem.at[1])
    total_copy.start()
    each(n_line, lambda k: line_copy(line, on_line(k)).wait_send())

    def sent(at, carry):
        each(n_grp, lambda k: grp_copy(at, grp, on_grp(k)).wait_send())
        return carry

    lax.fori_loop(0, n_line, sent, 0)

    def settle(origin, carry):
        if n_core > 1:
            core_copy(core, origin).wait_send()
        for owner in range(n_core):
            keep(owner, origin).wait()
        return carry

    lax.fori_loop(0, n_grp, settle, 0)
    own_copy.wait()
    total_copy.wait()


def finish(
    rows, batch,
    beyond_hbm, total_hbm, own_hbm,
    pos_vel_hbm, acc_jerk_hbm, pot_hbm,
    beyond, total, own, act, packed, more, pos_vel_ref, acc_jerk_ref, pot_ref, load_sem, store_sem,
):
    n, n_beyond = beyond.shape[0], beyond.shape[1]
    loads = [
        pltpu.make_async_copy(there, here, load_sem.at[i])
        for i, (there, here) in enumerate(((own_hbm, own), (beyond_hbm, beyond), (total_hbm, total)))
    ]
    for load in loads:
        load.start()
    lane = lax.broadcasted_iota(jnp.int32, (8, LANES), 1)
    row = lax.broadcasted_iota(jnp.int32, (8, LANES), 0)
    more[...] = jnp.zeros_like(more)
    loads[0].wait()
    spread(own, act)
    loads[1].wait()

    unroll = math.gcd(8, n)

    def pack(turn, carry):
        filled, now = carry
        counts = [beyond[turn * unroll + b, 0, 7, 0].astype(jnp.int32) for b in range(unroll)]
        for b in range(unroll):
            for chunk in range(n_beyond):
                many = jnp.minimum(jnp.maximum(counts[b] - (chunk + 1) * LANES, 0), LANES)
                start = lax.rem(filled, LANES)
                moved = pltpu.roll(beyond[turn * unroll + b, chunk], start, 1)
                now = jnp.where(lane >= start, moved, now)
                packed[filled // LANES] = now
                now = jnp.where(start + many >= LANES, moved, now)
                filled = filled + many
        return filled, now

    filled, now = lax.fori_loop(
        0, n // unroll, pack, (jnp.int32(0), jnp.zeros((8, LANES), jnp.float32))
    )
    last = filled // LANES
    packed[last] = jnp.where((row == 6) & (lane >= lax.rem(filled, LANES)), 0.0, now)
    for b in range(1, batch):
        packed[last + b] = jnp.zeros((8, LANES), jnp.float32)

    def turns(turn, carry):
        sweep(act, more, rows, [
            lambda c, at=turn * batch + b: packed[at, c : c + 1, :] for b in range(batch)
        ])
        return carry

    lax.fori_loop(0, (filled + batch * LANES - 1) // (batch * LANES), turns, 0)

    loads[2].wait()
    for c in range(6):
        acc_jerk_ref[c : c + 1, :] = jnp.sum((total[c] + more[c]).T, axis=0, keepdims=True)
    pot_ref[...] = -jnp.sum((total[6] + more[6]).T, axis=0, keepdims=True)
    stores = [
        pltpu.make_async_copy(here, there, store_sem.at[i])
        for i, (here, there) in enumerate((
            (acc_jerk_ref, acc_jerk_hbm), (pot_ref, pot_hbm), (pos_vel_ref, pos_vel_hbm),
        ))
    ]
    stores[0].start()
    stores[1].start()

    acc_end, jerk_end = acc_jerk_ref[0:3, :], acc_jerk_ref[3:6, :]
    pos_now, vel_now = own[0:3, :], own[3:6, :]
    acc_start, jerk_start, h = own[8:11, :], own[11:14, :], own[14:15, :]
    differ = acc_start - acc_end
    fourth = -6.0 * differ - h * (4.0 * jerk_start + 2.0 * jerk_end)
    fifth = 12.0 * differ + 6.0 * h * (jerk_start + jerk_end)
    pos_vel_ref[0:3, :] = pos_now + h * h * (1.0 / 24.0) * fourth + h * h * (1.0 / 120.0) * fifth
    pos_vel_ref[3:6, :] = vel_now + h * (1.0 / 6.0) * fourth + h * (1.0 / 24.0) * fifth
    stores[2].start()
    for store in stores:
        store.wait()


def solution(mesh):
    n_grp, n_dev = mesh.shape["grp"], mesh.shape["dev"]
    n = n_grp * n_dev

    def shards(positions, velocities, accel_old, jerk_old, masses, levels, live_count, active_slot):
        n_src, n_act = positions.shape[1], active_slot.shape[0]
        n_chunk = n_src // LANES
        hbm = pl.BlockSpec(memory_space=pltpu.HBM)
        args = (
            positions, velocities, accel_old, jerk_old,
            masses[None], levels[None], live_count, active_slot[None],
        )
        f32 = jnp.float32
        n_core = math.gcd(2, n_dev)
        n_line = n_dev // n_core
        dma = pltpu.SemaphoreType.DMA
        beyond, total, own = pl.pallas_call(
            functools.partial(
                share, n_grp, n_line, n_core, math.gcd(16, n_act), math.gcd(4, n_line)
            ),
            out_shape=(
                jax.ShapeDtypeStruct((n_core, n_grp, n_line, n_chunk - 1, 8, LANES), f32),
                jax.ShapeDtypeStruct((7, n_act, LANES), f32),
                jax.ShapeDtypeStruct((16, n_act), f32),
            ),
            in_specs=[hbm] * 8,
            out_specs=(hbm,) * 3,
            scratch_shapes=[
                (pltpu.SMEM if a is live_count else pltpu.VMEM)(a.shape, a.dtype) for a in args
            ] + [
                pltpu.VMEM((n_core, n_grp, n_line, n_chunk, 8, LANES), f32),
                pltpu.VMEM((6, n_act, LANES), f32),
                pltpu.VMEM((7, n_act, LANES), f32),
                pltpu.VMEM((16, n_act), f32),
                pltpu.VMEM((8, n_src), f32),
                dma((8,)),
                dma((n_line,)), dma((n_line,)),
                dma((n_line, n_grp)), dma((n_line, n_grp)),
                dma((n_grp,)), dma((n_grp,)),
                dma((n_core, n_grp)),
                dma((2,)),
            ],
            compiler_params=pltpu.CompilerParams(
                collective_id=0, has_side_effects=True, vmem_limit_bytes=60 * 1024 * 1024
            ),
        )(*args)
        batch = 4
        pos_vel, acc_jerk, pot = pl.pallas_call(
            functools.partial(finish, math.gcd(16, n_act), batch),
            out_shape=(
                jax.ShapeDtypeStruct((6, n_act), f32),
                jax.ShapeDtypeStruct((6, n_act), f32),
                jax.ShapeDtypeStruct((1, n_act), f32),
            ),
            in_specs=[hbm] * 3,
            out_specs=(hbm,) * 3,
            scratch_shapes=[
                pltpu.VMEM((n, n_chunk - 1, 8, LANES), f32),
                pltpu.VMEM((7, n_act, LANES), f32),
                pltpu.VMEM((16, n_act), f32),
                pltpu.VMEM((6, n_act, LANES), f32),
                pltpu.VMEM((n * (n_chunk - 1) + batch, 8, LANES), f32),
                pltpu.VMEM((7, n_act, LANES), f32),
                pltpu.VMEM((6, n_act), f32),
                pltpu.VMEM((6, n_act), f32),
                pltpu.VMEM((1, n_act), f32),
                dma((3,)),
                dma((3,)),
            ],
            compiler_params=pltpu.CompilerParams(vmem_limit_bytes=60 * 1024 * 1024),
        )(beyond.reshape(n, n_chunk - 1, 8, LANES), total, own)
        return pos_vel, acc_jerk, pot[0]

    split = P(None, ("grp", "dev"))
    flat = P(("grp", "dev"))
    return jax.shard_map(
        shards,
        mesh=mesh,
        in_specs=(split, split, split, split, flat, flat, flat, flat),
        out_specs=(split, split, flat),
        check_vma=False,
    )
```

```python
import functools
import math

import jax
import jax.numpy as jnp
from jax import lax
from jax.experimental import pallas as pl
from jax.experimental.pallas import tpu as pltpu
from jax.sharding import PartitionSpec as P

MESH = pl.DeviceIdType.MESH
LANES = 128
TAU_BASE = 0.5
SOFTEN_SQ = 0.0001


def add_pairs(state, sums, source):
    x, y, z, vx, vy, vz = state
    ax, ay, az, jx, jy, jz, pot = sums
    sx, sy, sz, svx, svy, svz, mass = source
    dx, dy, dz = sx - x, sy - y, sz - z
    ex, ey, ez = svx - vx, svy - vy, svz - vz
    inv = lax.rsqrt(dx * dx + dy * dy + dz * dz + SOFTEN_SQ)
    inv_sq = inv * inv
    w = mass * inv
    u = w * inv_sq
    radial = (3.0 * inv_sq) * (dx * ex + dy * ey + dz * ez)
    px, py, pz = u * dx, u * dy, u * dz
    return (
        ax + px, ay + py, az + pz,
        jx + (u * ex - radial * px), jy + (u * ey - radial * py), jz + (u * ez - radial * pz),
        pot + w,
    )


def sweep(act, total, rows, chunks):
    def group(g, carry):
        at = pl.ds(pl.multiple_of(g * rows, rows), rows)
        state = [act[c, at, :] for c in range(6)]
        sums = tuple(total[c, at, :] for c in range(7))
        for chunk in chunks:
            sums = add_pairs(state, sums, [chunk(c) for c in range(7)])
        for c in range(7):
            total[c, at, :] = sums[c]
        return carry

    lax.fori_loop(0, act.shape[1] // rows, group, 0)


def spread(own, act):
    for c in range(6):
        act[c] = jnp.broadcast_to(own[c : c + 1, :], (LANES, own.shape[1])).T


def share(
    n_grp, n_line, n_core, rows, batch,
    pos_hbm, vel_hbm, acc_hbm, jerk_hbm, mass_hbm, level_hbm, live_hbm, slot_hbm,
    beyond_hbm, total_hbm, own_hbm,
    pos_ref, vel_ref, acc_ref, jerk_ref, mass_ref, level_ref, live_ref, slot_ref,
    src, act, total, own, rest,
    load_sem, line_send, line_recv, grp_send, grp_recv, core_send, core_recv, beyond_sem, out_sem,
):
    n_src = pos_ref.shape[1]
    n_act = slot_ref.shape[1]
    n_chunk = n_src // LANES
    grp = lax.axis_index("grp")
    dev = lax.axis_index("dev")
    line, core = dev // n_core, lax.rem(dev, n_core)
    twin = n_core - 1 - core

    loads = [
        pltpu.make_async_copy(there, here, load_sem.at[i])
        for i, (there, here) in enumerate((
            (pos_hbm, pos_ref), (vel_hbm, vel_ref), (acc_hbm, acc_ref), (jerk_hbm, jerk_ref),
            (mass_hbm, mass_ref), (level_hbm, level_ref), (live_hbm, live_ref), (slot_hbm, slot_ref),
        ))
    ]
    for load in loads:
        load.start()

    def on_line(k):
        return lax.rem(line + k, n_line)

    def on_grp(k):
        return lax.rem(grp + k, n_grp)

    def each(count, body):
        def one(k, carry):
            body(k)
            return carry

        lax.fori_loop(1, count, one, 0)

    barrier = pltpu.get_barrier_semaphore()

    def greet(place):
        pl.semaphore_signal(barrier, inc=1, device_id=place, device_id_type=MESH)

    each(n_line, lambda k: greet((grp, on_line(k) * n_core + core)))
    each(n_grp, lambda k: greet((on_grp(k), dev)))
    if n_core > 1:
        greet((grp, line * n_core + twin))
    total[...] = jnp.zeros_like(total)
    for load in loads:
        load.wait()

    mine = src.at[core, grp, line]
    level = level_ref[...]
    step = jnp.full(level.shape, TAU_BASE, jnp.float32)
    step = jnp.where((level & 1) != 0, step * 0.5, step)
    step = jnp.where((level & 2) != 0, step * 0.25, step)
    step = jnp.where((level & 4) != 0, step * 0.0625, step)
    vel, acc, jerk = vel_ref[...], acc_ref[...], jerk_ref[...]
    pos_pred = pos_ref[...] + step * (vel + step * (acc * 0.5 + step * jerk * (1.0 / 6.0)))
    vel_pred = vel + step * (acc + step * jerk * 0.5)
    lane = lax.broadcasted_iota(jnp.int32, (1, n_src), 1)
    live = jnp.full((1, n_src), live_ref[0], jnp.int32)
    live_mass = jnp.where(lane < live, mass_ref[...], 0.0)
    count = live.astype(jnp.float32)
    for chunk in range(n_chunk):
        cut = slice(chunk * LANES, (chunk + 1) * LANES)
        mine[chunk, 0:3, :] = pos_pred[:, cut]
        mine[chunk, 3:6, :] = vel_pred[:, cut]
        mine[chunk, 6:7, :] = live_mass[:, cut]
        mine[chunk, 7:8, :] = count[:, cut]
    rest[0:3, :] = acc
    rest[3:6, :] = jerk
    rest[6:7, :] = step
    rest[7:8, :] = jnp.zeros_like(step)

    pl.semaphore_wait(barrier, (n_line - 1) + (n_grp - 1) + (n_core - 1))

    def line_copy(origin, other):
        block = src.at[core, grp, origin]
        return pltpu.make_async_remote_copy(
            src_ref=block, dst_ref=block,
            send_sem=line_send.at[other], recv_sem=line_recv.at[origin],
            device_id=(grp, other * n_core + core), device_id_type=MESH,
        )

    def grp_copy(at, origin, other):
        block = src.at[core, origin, at]
        return pltpu.make_async_remote_copy(
            src_ref=block, dst_ref=block,
            send_sem=grp_send.at[at, other], recv_sem=grp_recv.at[at, origin],
            device_id=(other, dev), device_id_type=MESH,
        )

    def to_groups(at):
        each(n_grp, lambda k: grp_copy(at, grp, on_grp(k)).start())

    def core_copy(owner, origin):
        block = src.at[owner, origin]
        return pltpu.make_async_remote_copy(
            src_ref=block, dst_ref=block,
            send_sem=core_send.at[origin], recv_sem=core_recv.at[origin],
            device_id=(grp, line * n_core + twin), device_id_type=MESH,
        )

    def keep(owner, origin):
        return pltpu.make_async_copy(
            src.at[owner, origin, :, 1:], beyond_hbm.at[owner, origin], beyond_sem.at[owner, origin]
        )

    def add(owner, origin):
        def turn(t, carry):
            sweep(act, total, rows, [
                lambda c, at=t * batch + b: src[owner, origin, at, 0, c : c + 1, :]
                for b in range(batch)
            ])
            return carry

        lax.fori_loop(0, n_line // batch, turn, 0)

    each(n_line, lambda k: line_copy(line, on_line(k)).start())
    to_groups(line)

    slot = jnp.broadcast_to(slot_ref[...], (8, n_act))
    low, part = slot & (LANES - 1), slot // LANES

    def pick(chunk_of):
        out = jnp.zeros((8, n_act), jnp.float32)
        for chunk in range(n_chunk):
            found = jnp.take_along_axis(chunk_of(chunk), low, axis=1)
            out = jnp.where(part == chunk, found, out)
        return out

    state = pick(lambda chunk: mine[chunk])
    own[0:8, :] = state
    own[8:16, :] = pick(lambda chunk: rest[:, chunk * LANES : (chunk + 1) * LANES])
    own_copy = pltpu.make_async_copy(own, own_hbm, out_sem.at[0])
    own_copy.start()
    spread(own, act)

    def add_near(ks):
        sweep(act, total, rows, [
            lambda c, at=on_line(k), chunk=chunk: src[core, grp, at, chunk, c : c + 1, :]
            for k in ks for chunk in range(n_chunk)
        ])

    near = min(n_line, batch)
    add_near([0])

    def pass_on(k):
        line_copy(on_line(k), on_line(k)).wait_recv()
        to_groups(on_line(k))

    each(n_line, pass_on)
    if n_core > 1:
        core_copy(core, grp).start()
    keep(core, grp).start()
    add_near(range(1, near))
    if n_line > near:
        def further(k, carry):
            add_near([k])
            return carry

        lax.fori_loop(near, n_line, further, 0)
    if n_core > 1:
        core_copy(twin, grp).wait_recv()
        keep(twin, grp).start()
        add(twin, grp)

    def forward(k):
        origin = on_grp(k)
        grp_copy(line, origin, origin).wait_recv()
        each(n_line, lambda at: grp_copy(on_line(at), origin, origin).wait_recv())
        if n_core > 1:
            core_copy(core, origin).start()
        keep(core, origin).start()

    each(n_grp, forward)
    each(n_grp, lambda k: add(core, on_grp(k)))

    if n_core > 1:
        def last(k):
            origin = on_grp(k)
            core_copy(twin, origin).wait_recv()
            keep(twin, origin).start()
            add(twin, origin)

        each(n_grp, last)

    total_copy = pltpu.make_async_copy(total, total_hbm, out_sem.at[1])
    total_copy.start()
    each(n_line, lambda k: line_copy(line, on_line(k)).wait_send())

    def sent(at, carry):
        each(n_grp, lambda k: grp_copy(at, grp, on_grp(k)).wait_send())
        return carry

    lax.fori_loop(0, n_line, sent, 0)

    def settle(origin, carry):
        if n_core > 1:
            core_copy(core, origin).wait_send()
        for owner in range(n_core):
            keep(owner, origin).wait()
        return carry

    lax.fori_loop(0, n_grp, settle, 0)
    own_copy.wait()
    total_copy.wait()


def finish(
    n_grp, n_line, n_core, rows, batch,
    beyond_hbm, total_hbm, own_hbm,
    pos_vel_hbm, acc_jerk_hbm, pot_hbm,
    beyond, total, own, act, packed, more, pos_vel_ref, acc_jerk_ref, pot_ref, load_sem, store_sem,
):
    n, n_beyond = beyond.shape[0], beyond.shape[1]
    loads = [
        pltpu.make_async_copy(there, here, load_sem.at[i])
        for i, (there, here) in enumerate(((own_hbm, own), (beyond_hbm, beyond), (total_hbm, total)))
    ]
    for load in loads:
        load.start()
    lane = lax.broadcasted_iota(jnp.int32, (8, LANES), 1)
    row = lax.broadcasted_iota(jnp.int32, (8, LANES), 0)
    more[...] = jnp.zeros_like(more)
    loads[0].wait()
    spread(own, act)
    loads[1].wait()

    unroll = math.gcd(8, n)

    near = (lax.rem(lax.axis_index("dev"), n_core) * n_grp + lax.axis_index("grp")) * n_line

    def pack(turn, carry):
        filled, now = carry
        counts = [beyond[turn * unroll + b, 0, 7, 0].astype(jnp.int32) for b in range(unroll)]
        for b in range(unroll):
            at = turn * unroll + b
            counts[b] = jnp.where((at >= near) & (at < near + n_line), 0, counts[b])
            for chunk in range(n_beyond):
                many = jnp.minimum(jnp.maximum(counts[b] - (chunk + 1) * LANES, 0), LANES)
                start = lax.rem(filled, LANES)
                moved = pltpu.roll(beyond[turn * unroll + b, chunk], start, 1)
                now = jnp.where(lane >= start, moved, now)
                packed[filled // LANES] = now
                now = jnp.where(start + many >= LANES, moved, now)
                filled = filled + many
        return filled, now

    filled, now = lax.fori_loop(
        0, n // unroll, pack, (jnp.int32(0), jnp.zeros((8, LANES), jnp.float32))
    )
    last = filled // LANES
    packed[last] = jnp.where((row == 6) & (lane >= lax.rem(filled, LANES)), 0.0, now)
    for b in range(1, batch):
        packed[last + b] = jnp.zeros((8, LANES), jnp.float32)

    def turns(turn, carry):
        sweep(act, more, rows, [
            lambda c, at=turn * batch + b: packed[at, c : c + 1, :] for b in range(batch)
        ])
        return carry

    lax.fori_loop(0, (filled + batch * LANES - 1) // (batch * LANES), turns, 0)

    loads[2].wait()
    for c in range(6):
        acc_jerk_ref[c : c + 1, :] = jnp.sum((total[c] + more[c]).T, axis=0, keepdims=True)
    pot_ref[...] = -jnp.sum((total[6] + more[6]).T, axis=0, keepdims=True)
    stores = [
        pltpu.make_async_copy(here, there, store_sem.at[i])
        for i, (here, there) in enumerate((
            (acc_jerk_ref, acc_jerk_hbm), (pot_ref, pot_hbm), (pos_vel_ref, pos_vel_hbm),
        ))
    ]
    stores[0].start()
    stores[1].start()

    acc_end, jerk_end = acc_jerk_ref[0:3, :], acc_jerk_ref[3:6, :]
    pos_now, vel_now = own[0:3, :], own[3:6, :]
    acc_start, jerk_start, h = own[8:11, :], own[11:14, :], own[14:15, :]
    differ = acc_start - acc_end
    fourth = -6.0 * differ - h * (4.0 * jerk_start + 2.0 * jerk_end)
    fifth = 12.0 * differ + 6.0 * h * (jerk_start + jerk_end)
    pos_vel_ref[0:3, :] = pos_now + h * h * (1.0 / 24.0) * fourth + h * h * (1.0 / 120.0) * fifth
    pos_vel_ref[3:6, :] = vel_now + h * (1.0 / 6.0) * fourth + h * (1.0 / 24.0) * fifth
    stores[2].start()
    for store in stores:
        store.wait()


def solution(mesh):
    n_grp, n_dev = mesh.shape["grp"], mesh.shape["dev"]
    n = n_grp * n_dev

    def shards(positions, velocities, accel_old, jerk_old, masses, levels, live_count, active_slot):
        n_src, n_act = positions.shape[1], active_slot.shape[0]
        n_chunk = n_src // LANES
        hbm = pl.BlockSpec(memory_space=pltpu.HBM)
        args = (
            positions, velocities, accel_old, jerk_old,
            masses[None], levels[None], live_count, active_slot[None],
        )
        f32 = jnp.float32
        n_core = math.gcd(2, n_dev)
        n_line = n_dev // n_core
        dma = pltpu.SemaphoreType.DMA
        beyond, total, own = pl.pallas_call(
            functools.partial(
                share, n_grp, n_line, n_core, math.gcd(16, n_act), math.gcd(4, n_line)
            ),
            out_shape=(
                jax.ShapeDtypeStruct((n_core, n_grp, n_line, n_chunk - 1, 8, LANES), f32),
                jax.ShapeDtypeStruct((7, n_act, LANES), f32),
                jax.ShapeDtypeStruct((16, n_act), f32),
            ),
            in_specs=[hbm] * 8,
            out_specs=(hbm,) * 3,
            scratch_shapes=[
                (pltpu.SMEM if a is live_count else pltpu.VMEM)(a.shape, a.dtype) for a in args
            ] + [
                pltpu.VMEM((n_core, n_grp, n_line, n_chunk, 8, LANES), f32),
                pltpu.VMEM((6, n_act, LANES), f32),
                pltpu.VMEM((7, n_act, LANES), f32),
                pltpu.VMEM((16, n_act), f32),
                pltpu.VMEM((8, n_src), f32),
                dma((8,)),
                dma((n_line,)), dma((n_line,)),
                dma((n_line, n_grp)), dma((n_line, n_grp)),
                dma((n_grp,)), dma((n_grp,)),
                dma((n_core, n_grp)),
                dma((2,)),
            ],
            compiler_params=pltpu.CompilerParams(
                collective_id=0, has_side_effects=True, vmem_limit_bytes=60 * 1024 * 1024
            ),
        )(*args)
        batch = 2
        pos_vel, acc_jerk, pot = pl.pallas_call(
            functools.partial(finish, n_grp, n_line, n_core, math.gcd(32, n_act), batch),
            out_shape=(
                jax.ShapeDtypeStruct((6, n_act), f32),
                jax.ShapeDtypeStruct((6, n_act), f32),
                jax.ShapeDtypeStruct((1, n_act), f32),
            ),
            in_specs=[hbm] * 3,
            out_specs=(hbm,) * 3,
            scratch_shapes=[
                pltpu.VMEM((n, n_chunk - 1, 8, LANES), f32),
                pltpu.VMEM((7, n_act, LANES), f32),
                pltpu.VMEM((16, n_act), f32),
                pltpu.VMEM((6, n_act, LANES), f32),
                pltpu.VMEM((n * (n_chunk - 1) + batch, 8, LANES), f32),
                pltpu.VMEM((7, n_act, LANES), f32),
                pltpu.VMEM((6, n_act), f32),
                pltpu.VMEM((6, n_act), f32),
                pltpu.VMEM((1, n_act), f32),
                dma((3,)),
                dma((3,)),
            ],
            compiler_params=pltpu.CompilerParams(vmem_limit_bytes=60 * 1024 * 1024),
        )(beyond.reshape(n, n_chunk - 1, 8, LANES), total, own)
        return pos_vel, acc_jerk, pot[0]

    split = P(None, ("grp", "dev"))
    flat = P(("grp", "dev"))
    return jax.shard_map(
        shards,
        mesh=mesh,
        in_specs=(split, split, split, split, flat, flat, flat, flat),
        out_specs=(split, split, flat),
        check_vma=False,
    )
```

```python
import functools
import math

import jax
import jax.numpy as jnp
from jax import lax
from jax.experimental import pallas as pl
from jax.experimental.pallas import tpu as pltpu
from jax.sharding import PartitionSpec as P

MESH = pl.DeviceIdType.MESH
LANES = 128
TAU_BASE = 0.5
SOFTEN_SQ = 0.0001


def add_pairs(state, sums, source):
    x, y, z, vx, vy, vz = state
    ax, ay, az, jx, jy, jz, pot = sums
    sx, sy, sz, svx, svy, svz, mass = source
    dx, dy, dz = sx - x, sy - y, sz - z
    ex, ey, ez = svx - vx, svy - vy, svz - vz
    inv = lax.rsqrt(dx * dx + dy * dy + dz * dz + SOFTEN_SQ)
    inv_sq = inv * inv
    w = mass * inv
    u = w * inv_sq
    radial = (3.0 * inv_sq) * (dx * ex + dy * ey + dz * ez)
    px, py, pz = u * dx, u * dy, u * dz
    return (
        ax + px, ay + py, az + pz,
        jx + (u * ex - radial * px), jy + (u * ey - radial * py), jz + (u * ez - radial * pz),
        pot + w,
    )


def sweep(act, total, rows, chunks):
    def group(g, carry):
        at = pl.ds(pl.multiple_of(g * rows, rows), rows)
        state = [act[c, at, :] for c in range(6)]
        sums = tuple(total[c, at, :] for c in range(7))
        for chunk in chunks:
            sums = add_pairs(state, sums, [chunk(c) for c in range(7)])
        for c in range(7):
            total[c, at, :] = sums[c]
        return carry

    lax.fori_loop(0, act.shape[1] // rows, group, 0)


def spread(own, act):
    for c in range(6):
        act[c] = jnp.broadcast_to(own[c : c + 1, :], (LANES, own.shape[1])).T


def share(
    n_grp, n_line, n_core, rows, batch,
    pos_hbm, vel_hbm, acc_hbm, jerk_hbm, mass_hbm, level_hbm, live_hbm, slot_hbm,
    beyond_hbm, total_hbm, own_hbm,
    pos_ref, vel_ref, acc_ref, jerk_ref, mass_ref, level_ref, live_ref, slot_ref,
    src, act, total, own, rest,
    load_sem, line_send, line_recv, grp_send, grp_recv, core_send, core_recv, beyond_sem, out_sem,
):
    n_src = pos_ref.shape[1]
    n_act = slot_ref.shape[1]
    n_chunk = n_src // LANES
    grp = lax.axis_index("grp")
    dev = lax.axis_index("dev")
    line, core = dev // n_core, lax.rem(dev, n_core)
    twin = n_core - 1 - core

    loads = [
        pltpu.make_async_copy(there, here, load_sem.at[i])
        for i, (there, here) in enumerate((
            (pos_hbm, pos_ref), (vel_hbm, vel_ref), (acc_hbm, acc_ref), (jerk_hbm, jerk_ref),
            (mass_hbm, mass_ref), (level_hbm, level_ref), (live_hbm, live_ref), (slot_hbm, slot_ref),
        ))
    ]
    for load in loads:
        load.start()

    def on_line(k):
        return lax.rem(line + k, n_line)

    def on_grp(k):
        return lax.rem(grp + k, n_grp)

    def each(count, body):
        def one(k, carry):
            body(k)
            return carry

        lax.fori_loop(1, count, one, 0)

    barrier = pltpu.get_barrier_semaphore()

    def greet(place):
        pl.semaphore_signal(barrier, inc=1, device_id=place, device_id_type=MESH)

    each(n_line, lambda k: greet((grp, on_line(k) * n_core + core)))
    each(n_grp, lambda k: greet((on_grp(k), dev)))
    if n_core > 1:
        greet((grp, line * n_core + twin))
    total[...] = jnp.zeros_like(total)
    for load in loads:
        load.wait()

    mine = src.at[core, grp, line]
    level = level_ref[...]
    step = jnp.full(level.shape, TAU_BASE, jnp.float32)
    step = jnp.where((level & 1) != 0, step * 0.5, step)
    step = jnp.where((level & 2) != 0, step * 0.25, step)
    step = jnp.where((level & 4) != 0, step * 0.0625, step)
    vel, acc, jerk = vel_ref[...], acc_ref[...], jerk_ref[...]
    pos_pred = pos_ref[...] + step * (vel + step * (acc * 0.5 + step * jerk * (1.0 / 6.0)))
    vel_pred = vel + step * (acc + step * jerk * 0.5)
    lane = lax.broadcasted_iota(jnp.int32, (1, n_src), 1)
    live = jnp.full((1, n_src), live_ref[0], jnp.int32)
    live_mass = jnp.where(lane < live, mass_ref[...], 0.0)
    count = live.astype(jnp.float32)
    for chunk in range(n_chunk):
        cut = slice(chunk * LANES, (chunk + 1) * LANES)
        mine[chunk, 0:3, :] = pos_pred[:, cut]
        mine[chunk, 3:6, :] = vel_pred[:, cut]
        mine[chunk, 6:7, :] = live_mass[:, cut]
        mine[chunk, 7:8, :] = count[:, cut]
    rest[0:3, :] = acc
    rest[3:6, :] = jerk
    rest[6:7, :] = step
    rest[7:8, :] = jnp.zeros_like(step)

    pl.semaphore_wait(barrier, (n_line - 1) + (n_grp - 1) + (n_core - 1))

    def line_copy(origin, other):
        block = src.at[core, grp, origin]
        return pltpu.make_async_remote_copy(
            src_ref=block, dst_ref=block,
            send_sem=line_send.at[other], recv_sem=line_recv.at[origin],
            device_id=(grp, other * n_core + core), device_id_type=MESH,
        )

    def grp_copy(at, origin, other):
        block = src.at[core, origin, at]
        return pltpu.make_async_remote_copy(
            src_ref=block, dst_ref=block,
            send_sem=grp_send.at[at, other], recv_sem=grp_recv.at[at, origin],
            device_id=(other, dev), device_id_type=MESH,
        )

    def to_groups(at):
        each(n_grp, lambda k: grp_copy(at, grp, on_grp(k)).start())

    def core_copy(owner, origin):
        block = src.at[owner, origin]
        return pltpu.make_async_remote_copy(
            src_ref=block, dst_ref=block,
            send_sem=core_send.at[origin], recv_sem=core_recv.at[origin],
            device_id=(grp, line * n_core + twin), device_id_type=MESH,
        )

    def keep(owner, origin):
        return pltpu.make_async_copy(
            src.at[owner, origin, :, 1:], beyond_hbm.at[owner, origin], beyond_sem.at[owner, origin]
        )

    def add(owner, origin):
        def turn(t, carry):
            sweep(act, total, rows, [
                lambda c, at=t * batch + b: src[owner, origin, at, 0, c : c + 1, :]
                for b in range(batch)
            ])
            return carry

        lax.fori_loop(0, n_line // batch, turn, 0)

    each(n_line, lambda k: line_copy(line, on_line(k)).start())
    to_groups(line)

    slot = jnp.broadcast_to(slot_ref[...], (8, n_act))
    low, part = slot & (LANES - 1), slot // LANES

    def pick(chunk_of):
        out = jnp.zeros((8, n_act), jnp.float32)
        for chunk in range(n_chunk):
            found = jnp.take_along_axis(chunk_of(chunk), low, axis=1)
            out = jnp.where(part == chunk, found, out)
        return out

    state = pick(lambda chunk: mine[chunk])
    own[0:8, :] = state
    own[8:16, :] = pick(lambda chunk: rest[:, chunk * LANES : (chunk + 1) * LANES])
    own_copy = pltpu.make_async_copy(own, own_hbm, out_sem.at[0])
    own_copy.start()
    spread(own, act)

    def add_near(ks):
        sweep(act, total, rows, [
            lambda c, at=on_line(k), chunk=chunk: src[core, grp, at, chunk, c : c + 1, :]
            for k in ks for chunk in range(n_chunk)
        ])

    near = min(n_line, batch)
    add_near([0])

    def pass_on(k):
        line_copy(on_line(k), on_line(k)).wait_recv()
        to_groups(on_line(k))

    each(n_line, pass_on)
    if n_core > 1:
        core_copy(core, grp).start()
    keep(core, grp).start()
    add_near(range(1, near))
    if n_line > near:
        def further(k, carry):
            add_near([k])
            return carry

        lax.fori_loop(near, n_line, further, 0)
    if n_core > 1:
        core_copy(twin, grp).wait_recv()
        keep(twin, grp).start()
        add(twin, grp)

    def forward(k):
        origin = on_grp(k)
        grp_copy(line, origin, origin).wait_recv()
        each(n_line, lambda at: grp_copy(on_line(at), origin, origin).wait_recv())
        if n_core > 1:
            core_copy(core, origin).start()
        keep(core, origin).start()

    each(n_grp, forward)
    each(n_grp, lambda k: add(core, on_grp(k)))

    if n_core > 1:
        def last(k):
            origin = on_grp(k)
            core_copy(twin, origin).wait_recv()
            keep(twin, origin).start()
            add(twin, origin)

        each(n_grp, last)

    total_copy = pltpu.make_async_copy(total, total_hbm, out_sem.at[1])
    total_copy.start()
    each(n_line, lambda k: line_copy(line, on_line(k)).wait_send())

    def sent(at, carry):
        each(n_grp, lambda k: grp_copy(at, grp, on_grp(k)).wait_send())
        return carry

    lax.fori_loop(0, n_line, sent, 0)

    def settle(origin, carry):
        if n_core > 1:
            core_copy(core, origin).wait_send()
        for owner in range(n_core):
            keep(owner, origin).wait()
        return carry

    lax.fori_loop(0, n_grp, settle, 0)
    own_copy.wait()
    total_copy.wait()


def finish(
    n_grp, n_line, n_core, rows, batch,
    beyond_hbm, total_hbm, own_hbm,
    pos_vel_hbm, acc_jerk_hbm, pot_hbm,
    beyond, total, own, act, packed, more, pos_vel_ref, acc_jerk_ref, pot_ref, load_sem, store_sem,
):
    n, n_beyond = beyond.shape[0], beyond.shape[1]
    loads = [
        pltpu.make_async_copy(there, here, load_sem.at[i])
        for i, (there, here) in enumerate(((own_hbm, own), (beyond_hbm, beyond), (total_hbm, total)))
    ]
    for load in loads:
        load.start()
    lane = lax.broadcasted_iota(jnp.int32, (8, LANES), 1)
    row = lax.broadcasted_iota(jnp.int32, (8, LANES), 0)
    more[...] = jnp.zeros_like(more)
    loads[0].wait()
    spread(own, act)
    loads[1].wait()

    unroll = math.gcd(8, n)

    near = (lax.rem(lax.axis_index("dev"), n_core) * n_grp + lax.axis_index("grp")) * n_line

    def pack(turn, carry):
        filled, now = carry
        counts = [beyond[turn * unroll + b, 0, 7, 0].astype(jnp.int32) for b in range(unroll)]
        for b in range(unroll):
            at = turn * unroll + b
            counts[b] = jnp.where((at >= near) & (at < near + n_line), 0, counts[b])
            for chunk in range(n_beyond):
                many = jnp.minimum(jnp.maximum(counts[b] - (chunk + 1) * LANES, 0), LANES)
                start = lax.rem(filled, LANES)
                moved = pltpu.roll(beyond[turn * unroll + b, chunk], start, 1)
                now = jnp.where(lane >= start, moved, now)
                packed[filled // LANES] = now
                now = jnp.where(start + many >= LANES, moved, now)
                filled = filled + many
        return filled, now

    filled, now = lax.fori_loop(
        0, n // unroll, pack, (jnp.int32(0), jnp.zeros((8, LANES), jnp.float32))
    )
    last = filled // LANES
    packed[last] = jnp.where((row == 6) & (lane >= lax.rem(filled, LANES)), 0.0, now)
    for b in range(1, batch):
        packed[last + b] = jnp.zeros((8, LANES), jnp.float32)

    def turns(turn, carry):
        sweep(act, more, rows, [
            lambda c, at=turn * batch + b: packed[at, c : c + 1, :] for b in range(batch)
        ])
        return carry

    lax.fori_loop(0, (filled + batch * LANES - 1) // (batch * LANES), turns, 0)

    loads[2].wait()
    for c in range(6):
        acc_jerk_ref[c : c + 1, :] = jnp.sum((total[c] + more[c]).T, axis=0, keepdims=True)
    pot_ref[...] = -jnp.sum((total[6] + more[6]).T, axis=0, keepdims=True)
    stores = [
        pltpu.make_async_copy(here, there, store_sem.at[i])
        for i, (here, there) in enumerate((
            (acc_jerk_ref, acc_jerk_hbm), (pot_ref, pot_hbm), (pos_vel_ref, pos_vel_hbm),
        ))
    ]
    stores[0].start()
    stores[1].start()

    acc_end, jerk_end = acc_jerk_ref[0:3, :], acc_jerk_ref[3:6, :]
    pos_now, vel_now = own[0:3, :], own[3:6, :]
    acc_start, jerk_start, h = own[8:11, :], own[11:14, :], own[14:15, :]
    differ = acc_start - acc_end
    fourth = -6.0 * differ - h * (4.0 * jerk_start + 2.0 * jerk_end)
    fifth = 12.0 * differ + 6.0 * h * (jerk_start + jerk_end)
    pos_vel_ref[0:3, :] = pos_now + h * h * (1.0 / 24.0) * fourth + h * h * (1.0 / 120.0) * fifth
    pos_vel_ref[3:6, :] = vel_now + h * (1.0 / 6.0) * fourth + h * (1.0 / 24.0) * fifth
    stores[2].start()
    for store in stores:
        store.wait()


def solution(mesh):
    n_grp, n_dev = mesh.shape["grp"], mesh.shape["dev"]
    n = n_grp * n_dev

    def shards(positions, velocities, accel_old, jerk_old, masses, levels, live_count, active_slot):
        n_src, n_act = positions.shape[1], active_slot.shape[0]
        n_chunk = n_src // LANES
        hbm = pl.BlockSpec(memory_space=pltpu.HBM)
        args = (
            positions, velocities, accel_old, jerk_old,
            masses[None], levels[None], live_count, active_slot[None],
        )
        f32 = jnp.float32
        n_core = math.gcd(2, n_dev)
        n_line = n_dev // n_core
        dma = pltpu.SemaphoreType.DMA
        beyond, total, own = pl.pallas_call(
            functools.partial(
                share, n_grp, n_line, n_core, math.gcd(16, n_act), math.gcd(4, n_line)
            ),
            out_shape=(
                jax.ShapeDtypeStruct((n_core, n_grp, n_line, n_chunk - 1, 8, LANES), f32),
                jax.ShapeDtypeStruct((7, n_act, LANES), f32),
                jax.ShapeDtypeStruct((16, n_act), f32),
            ),
            in_specs=[hbm] * 8,
            out_specs=(hbm,) * 3,
            scratch_shapes=[
                (pltpu.SMEM if a is live_count else pltpu.VMEM)(a.shape, a.dtype) for a in args
            ] + [
                pltpu.VMEM((n_core, n_grp, n_line, n_chunk, 8, LANES), f32),
                pltpu.VMEM((6, n_act, LANES), f32),
                pltpu.VMEM((7, n_act, LANES), f32),
                pltpu.VMEM((16, n_act), f32),
                pltpu.VMEM((8, n_src), f32),
                dma((8,)),
                dma((n_line,)), dma((n_line,)),
                dma((n_line, n_grp)), dma((n_line, n_grp)),
                dma((n_grp,)), dma((n_grp,)),
                dma((n_core, n_grp)),
                dma((2,)),
            ],
            compiler_params=pltpu.CompilerParams(
                collective_id=0, has_side_effects=True, vmem_limit_bytes=60 * 1024 * 1024
            ),
        )(*args)
        batch = 4
        pos_vel, acc_jerk, pot = pl.pallas_call(
            functools.partial(finish, n_grp, n_line, n_core, math.gcd(16, n_act), batch),
            out_shape=(
                jax.ShapeDtypeStruct((6, n_act), f32),
                jax.ShapeDtypeStruct((6, n_act), f32),
                jax.ShapeDtypeStruct((1, n_act), f32),
            ),
            in_specs=[hbm] * 3,
            out_specs=(hbm,) * 3,
            scratch_shapes=[
                pltpu.VMEM((n, n_chunk - 1, 8, LANES), f32),
                pltpu.VMEM((7, n_act, LANES), f32),
                pltpu.VMEM((16, n_act), f32),
                pltpu.VMEM((6, n_act, LANES), f32),
                pltpu.VMEM((n * (n_chunk - 1) + batch, 8, LANES), f32),
                pltpu.VMEM((7, n_act, LANES), f32),
                pltpu.VMEM((6, n_act), f32),
                pltpu.VMEM((6, n_act), f32),
                pltpu.VMEM((1, n_act), f32),
                dma((3,)),
                dma((3,)),
            ],
            compiler_params=pltpu.CompilerParams(vmem_limit_bytes=60 * 1024 * 1024),
        )(beyond.reshape(n, n_chunk - 1, 8, LANES), total, own)
        return pos_vel, acc_jerk, pot[0]

    split = P(None, ("grp", "dev"))
    flat = P(("grp", "dev"))
    return jax.shard_map(
        shards,
        mesh=mesh,
        in_specs=(split, split, split, split, flat, flat, flat, flat),
        out_specs=(split, split, flat),
        check_vma=False,
    )
```
